32 devices in a mesh: lat: 8 (over y, x, core), lon: 4 (over z).
Axes of the slice: x: 2, y: 2, z: 4, core: 2. Of those that a mesh axis runs over, the one named last changes fastest.
Arguments:
- features: bfloat16 [512, 1024, 128], P('lat', 'lon'), may hold values from -6 to 6
- w_first: bfloat16 [2, 1, 128, 128], replicated, may hold values from -0.375 to 0.375
- bias_first: float32 [2, 1, 128], replicated, may hold values from -3 to 3
- w_second: bfloat16 [2, 1, 128, 128], replicated, may hold values from -0.375 to 0.375
- bias_second: float32 [2, 1, 128], replicated, may hold values from -0.3 to 0.3
Outputs:
- mixed_field: bfloat16 [512, 1024, 128], P('lat', 'lon')
The draws below stay inside these ranges and needn't reach their ends.
All inputs are finite; a program needn't handle non-finite values.
Results may differ from the reference program's by a relative error of at most 0.025.
Values may be sent and summed in bfloat16 or wider, within the bound.
No kernel may reach another device: no remote copies, remote signals or barrier semaphores. Data moves between devices by JAX's collectives and lax.ppermute only.
A program may use at most 128 MiB of HBM per device.

```python
import math
import jax
import jax.numpy as jnp
from jax import lax

NLAT = 512
NLON = 1024
BLOCK = 128
NBLK = 1
C = 128
N_LON = 4


def block_levels(rng, shape, pieces, least, top_value):
    def one(position, shards_of):
        steps = jax.random.uniform(jax.random.fold_in(jax.random.fold_in(rng, 6), position), (shards_of,), jnp.float32, least / len(pieces), top_value / len(pieces))
        return jnp.repeat(jnp.exp(steps), shape[position] // shards_of).reshape((-1,) + (1,) * (len(shape) - position - 1))

    level = one(*pieces[0])
    for cut in pieces[1:]:
        level = level * one(*cut)
    return level


def scatter_about(stream_key, shape, deviation, most, pieces=(), held_as=jnp.bfloat16):
    entries = jax.random.normal(stream_key, shape, jnp.float32) * deviation
    if len(pieces) > 0:
        entries = block_levels(stream_key, shape, pieces, -0.22, 0.18) * entries
    return jnp.clip(entries, min=-most, max=most).astype(held_as)


def setup_inputs(seed: int = 0) -> dict:
    seeds = jax.random.split(jax.random.key(seed), 6)
    features = scatter_about(seeds[0], (NLAT, NLON, C), 1.0, 6.0, ((0, 8), (1, 4)))
    w_first = scatter_about(seeds[1], (2, NBLK, BLOCK, BLOCK), (2 * BLOCK) ** -0.5, 0.375)
    bias_first = scatter_about(seeds[2], (2, NBLK, BLOCK), 0.5, 3.0, (), jnp.float32)
    w_second = scatter_about(seeds[3], (2, NBLK, BLOCK, BLOCK), (2 * BLOCK) ** -0.5, 0.375)
    bias_second = scatter_about(seeds[4], (2, NBLK, BLOCK), 0.05, 0.3, (), jnp.float32)
    return {"features": features, "w_first": w_first, "bias_first": bias_first, "w_second": w_second, "bias_second": bias_second}


shrink_level = 0.01

def to_half(values):
    rounded = values.astype(jnp.bfloat16)
    rounded = lax.optimization_barrier(rounded)
    return rounded.astype(jnp.float32)

def round_complex(values):
    return lax.complex(to_half(jnp.real(values)), to_half(jnp.imag(values)))

def phase_parts(product, length, sign):
    angle_value = (product % length).astype(jnp.float32) * (sign * 2.0 * math.pi / length)
    return (jnp.cos(angle_value), jnp.sin(angle_value))

def phase_factor(product, length, sign):
    cos_part, sin_part = phase_parts(product, length, sign)
    return lax.complex(cos_part, sin_part)

def bit_reverse(number, levels):
    result = jnp.zeros_like(number)
    for bit_level in range(levels):
        result = result + number // 2 ** bit_level % 2 * 2 ** (levels - 1 - bit_level)
    return result

def block_sections(values, levels):
    real_part = values
    imag_part = jnp.zeros_like(values)
    full_shape = values.shape
    for section_level in range(levels - 1, -1, -1):
        half_span = 2 ** section_level
        split_shape = (full_shape[0], full_shape[1] // (2 * half_span), 2, half_span) + full_shape[2:]
        real_split = real_part.reshape(split_shape)
        imag_split = imag_part.reshape(split_shape)
        tw_cos, tw_sin = phase_parts(jnp.arange(half_span, dtype=jnp.int32), 2 * half_span, -1.0)
        tw_cos = tw_cos[None, None, :, None, None]
        tw_sin = tw_sin[None, None, :, None, None]
        sum_re = real_split[:, :, 0] + real_split[:, :, 1]
        sum_im = imag_split[:, :, 0] + imag_split[:, :, 1]
        diff_re = real_split[:, :, 0] - real_split[:, :, 1]
        diff_im = imag_split[:, :, 0] - imag_split[:, :, 1]
        upper_re = diff_re * tw_cos - diff_im * tw_sin
        upper_im = diff_re * tw_sin + diff_im * tw_cos
        real_part = to_half(jnp.stack([sum_re, upper_re], axis=2).reshape(full_shape))
        imag_part = to_half(jnp.stack([sum_im, upper_im], axis=2).reshape(full_shape))
    return (real_part, imag_part)

def block_product(real_part, imag_part, weights):
    real_out = jnp.einsum('tnj,njk->tnk', real_part, weights[0]) - jnp.einsum('tnj,njk->tnk', imag_part, weights[1])
    imag_out = jnp.einsum('tnj,njk->tnk', imag_part, weights[0]) + jnp.einsum('tnj,njk->tnk', real_part, weights[1])
    return (real_out, imag_out)

def soft_shrink(values):
    return jnp.sign(values) * jnp.maximum(jnp.abs(values) - shrink_level, 0.0)

def spectral_mix(real_part, imag_part, first_w, first_bias, second_w, second_bias):
    shape_in = real_part.shape
    blocks = first_w.shape[1]
    block_width = first_w.shape[2]
    flat_re = real_part.astype(jnp.float32).reshape(-1, blocks, block_width)
    flat_im = imag_part.astype(jnp.float32).reshape(-1, blocks, block_width)
    hid_re, hid_im = block_product(flat_re, flat_im, first_w)
    act_re = to_half(jax.nn.relu(hid_re + first_bias[0]))
    act_im = to_half(jax.nn.relu(hid_im + first_bias[1]))
    out_re, out_im = block_product(act_re, act_im, second_w)
    return (soft_shrink(out_re + second_bias[0]).astype(jnp.bfloat16).reshape(shape_in), soft_shrink(out_im + second_bias[1]).astype(jnp.bfloat16).reshape(shape_in))

def forward_group(group):
    lat_cells, total_lon, group_width = group.shape
    shard_cells = total_lon // N_LON
    keep_cells = shard_cells // 2
    levels = N_LON.bit_length() - 1
    blocks = group.astype(jnp.float32).reshape(lat_cells, N_LON, shard_cells, group_width)
    sectioned_re, sectioned_im = block_sections(blocks, levels)
    order = bit_reverse(jnp.arange(N_LON, dtype=jnp.int32), levels)
    natural = lax.complex(jnp.take(sectioned_re, order, axis=1), jnp.take(sectioned_im, order, axis=1))
    product = jnp.arange(N_LON, dtype=jnp.int32)[:, None] * jnp.arange(shard_cells, dtype=jnp.int32)[None, :]
    first_pass = round_complex(natural * phase_factor(product, total_lon, -1.0)[None, :, :, None])
    lon_spectrum = round_complex(jnp.fft.fft(first_pass, axis=2)[:, :, :keep_cells])
    spectrum = round_complex(jnp.fft.fft(lon_spectrum, axis=0) / math.sqrt(lat_cells * total_lon))
    return (jnp.real(spectrum).astype(jnp.bfloat16), jnp.imag(spectrum).astype(jnp.bfloat16))

def inverse_group(pair):
    real_part, imag_part = pair
    lat_cells, shard_count, keep_cells, group_width = real_part.shape
    shard_cells = 2 * keep_cells
    total_lon = shard_count * shard_cells
    mixed = lax.complex(real_part.astype(jnp.float32), imag_part.astype(jnp.float32))
    lat_back = round_complex(jnp.fft.ifft(mixed, axis=0) * lat_cells)
    first_row = jnp.arange(shard_count, dtype=jnp.int32)[:, None] == 0
    first_col = jnp.arange(keep_cells, dtype=jnp.int32)[None, :] == 0
    weight = jnp.where(first_row & first_col, 1.0, 2.0).astype(jnp.float32)
    weighted = lat_back * weight[None, :, :, None]
    padded = jnp.pad(weighted, ((0, 0), (0, 0), (0, shard_cells - keep_cells), (0, 0)))
    over_q = jnp.fft.ifft(padded, axis=2) * shard_cells
    product = jnp.arange(shard_count, dtype=jnp.int32)[:, None] * jnp.arange(shard_cells, dtype=jnp.int32)[None, :]
    lon_back = round_complex(over_q * phase_factor(product, total_lon, 1.0)[None, :, :, None])
    over_p = jnp.fft.ifft(lon_back, axis=1) * shard_count
    filtered = jnp.real(over_p) / math.sqrt(lat_cells * total_lon)
    return filtered.astype(jnp.bfloat16).reshape(lat_cells, total_lon, group_width)

def reference(features, w_first, bias_first, w_second, bias_second):
    lat_cells, total_lon, channels = features.shape
    group_width = math.gcd(channels, 32)
    group_count = channels // group_width
    shard_cells = total_lon // N_LON
    keep_cells = shard_cells // 2
    stacked = jnp.moveaxis(features.reshape(lat_cells, total_lon, group_count, group_width), 2, 0)
    spec_re, spec_im = lax.map(forward_group, stacked)

    def regroup(parts):
        return jnp.moveaxis(parts, 0, 3).reshape(lat_cells, N_LON, keep_cells, channels)
    spec_re = regroup(spec_re)
    spec_im = regroup(spec_im)
    first_w = w_first.astype(jnp.float32)
    second_w = w_second.astype(jnp.float32)
    first_bias = bias_first.astype(jnp.float32)
    second_bias = bias_second.astype(jnp.float32)

    def mix_row(pair):
        return spectral_mix(pair[0], pair[1], first_w, first_bias, second_w, second_bias)
    mix_re, mix_im = lax.map(mix_row, (spec_re, spec_im))

    def split_groups(parts):
        return jnp.moveaxis(parts.reshape(lat_cells, N_LON, keep_cells, group_count, group_width), 3, 0)
    filtered = lax.map(inverse_group, (split_groups(mix_re), split_groups(mix_im)))
    filtered = jnp.moveaxis(filtered, 0, 2).reshape(lat_cells, total_lon, channels)
    return (features.astype(jnp.float32) + filtered.astype(jnp.float32)).astype(jnp.bfloat16)
```

```python
import math

import jax
import jax.numpy as jnp
import numpy as np
from jax import lax
from jax.experimental import pallas as pl
from jax.experimental.pallas import tpu as pltpu
from jax.sharding import PartitionSpec as P

shrink_level = 0.01


def phase_pair(product, length, sign):
    angle_value = (product % length).astype(jnp.float32) * (sign * 2.0 * math.pi / length)
    return (jnp.cos(angle_value), jnp.sin(angle_value))


def index_outer(left_index, right_index):
    return left_index[:, None] * right_index[None, :]


def twin_dot(pattern, operand, phase_table):
    upper_part = phase_table.astype(jnp.bfloat16)
    lower_part = (phase_table - upper_part.astype(jnp.float32)).astype(jnp.bfloat16)
    return jnp.einsum(
        pattern, operand, upper_part, preferred_element_type=jnp.float32
    ) + jnp.einsum(pattern, operand, lower_part, preferred_element_type=jnp.float32)


def complex_table(pattern, real_part, imag_part, cos_table, sin_table):
    real_out = twin_dot(pattern, real_part, cos_table) - twin_dot(pattern, imag_part, sin_table)
    imag_out = twin_dot(pattern, real_part, sin_table) + twin_dot(pattern, imag_part, cos_table)
    return (real_out, imag_out)


def bit_reverse(number, levels):
    result = jnp.zeros_like(number)
    for bit_level in range(levels):
        result = result + number // 2**bit_level % 2 * 2 ** (levels - 1 - bit_level)
    return result


def local_sections(received, levels):
    full_shape = received.shape
    real_part = received.astype(jnp.float32)
    imag_part = jnp.zeros_like(real_part)
    real_half = received
    imag_half = imag_part.astype(jnp.bfloat16)
    for section_level in range(levels - 1, -1, -1):
        half_span = 2**section_level
        split_shape = (full_shape[0], full_shape[1] // (2 * half_span), 2, half_span) + full_shape[
            2:
        ]
        real_split = real_part.reshape(split_shape)
        imag_split = imag_part.reshape(split_shape)
        tw_cos, tw_sin = phase_pair(jnp.arange(half_span, dtype=jnp.int32), 2 * half_span, -1.0)
        tw_cos = tw_cos[None, None, :, None, None]
        tw_sin = tw_sin[None, None, :, None, None]
        sum_re = real_split[:, :, 0] + real_split[:, :, 1]
        sum_im = imag_split[:, :, 0] + imag_split[:, :, 1]
        diff_re = real_split[:, :, 0] - real_split[:, :, 1]
        diff_im = imag_split[:, :, 0] - imag_split[:, :, 1]
        upper_re = diff_re * tw_cos - diff_im * tw_sin
        upper_im = diff_re * tw_sin + diff_im * tw_cos
        real_half = jnp.stack([sum_re, upper_re], axis=2).reshape(full_shape).astype(jnp.bfloat16)
        imag_half = jnp.stack([sum_im, upper_im], axis=2).reshape(full_shape).astype(jnp.bfloat16)
        real_part = real_half.astype(jnp.float32)
        imag_part = imag_half.astype(jnp.float32)
    return (real_half, imag_half)


def block_product(real_part, imag_part, weights):
    real_out = jnp.einsum(
        "tnj,njk->tnk", real_part, weights[0], preferred_element_type=jnp.float32
    ) - jnp.einsum("tnj,njk->tnk", imag_part, weights[1], preferred_element_type=jnp.float32)
    imag_out = jnp.einsum(
        "tnj,njk->tnk", imag_part, weights[0], preferred_element_type=jnp.float32
    ) + jnp.einsum("tnj,njk->tnk", real_part, weights[1], preferred_element_type=jnp.float32)
    return (real_out, imag_out)


def soft_shrink(values):
    return jnp.sign(values) * jnp.maximum(jnp.abs(values) - shrink_level, 0.0)


def spectral_mix(real_part, imag_part, w_first, bias_first, w_second, bias_second):
    shape_in = real_part.shape
    blocks = w_first.shape[1]
    block_width = w_first.shape[2]
    flat_re = real_part.reshape(-1, blocks, block_width)
    flat_im = imag_part.reshape(-1, blocks, block_width)
    hid_re, hid_im = block_product(flat_re, flat_im, w_first)
    act_re = jax.nn.relu(hid_re + bias_first[0]).astype(jnp.bfloat16)
    act_im = jax.nn.relu(hid_im + bias_first[1]).astype(jnp.bfloat16)
    out_re, out_im = block_product(act_re, act_im, w_second)
    return (
        soft_shrink(out_re + bias_second[0]).astype(jnp.bfloat16).reshape(shape_in),
        soft_shrink(out_im + bias_second[1]).astype(jnp.bfloat16).reshape(shape_in),
    )


def send_real(blocks):
    return lax.all_to_all(blocks, "lon", split_axis=1, concat_axis=1, tiled=True)


def to_columns(real_part, imag_part):
    return (
        lax.all_to_all(real_part, "lat", split_axis=1, concat_axis=0, tiled=True),
        lax.all_to_all(imag_part, "lat", split_axis=1, concat_axis=0, tiled=True),
    )


def to_rows(real_part, imag_part):
    return (
        lax.all_to_all(real_part, "lat", split_axis=0, concat_axis=1, tiled=True),
        lax.all_to_all(imag_part, "lat", split_axis=0, concat_axis=1, tiled=True),
    )


def general_body(features, w_first, bias_first, w_second, bias_second):
    lat_rows, lon_cells, channels = features.shape
    lon_count = lax.axis_size("lon")
    lat_count = lax.axis_size("lat")
    total_lat = lat_rows * lat_count
    total_lon = lon_cells * lon_count
    stride = lon_cells // lon_count
    keep_cells = lon_cells // 2
    norm_factor = 1.0 / math.sqrt(total_lat * total_lon)
    levels = lon_count.bit_length() - 1
    lon_place = lax.axis_index("lon")
    shard_index = jnp.arange(lon_count, dtype=jnp.int32)
    cell_index = jnp.arange(lon_cells, dtype=jnp.int32)
    keep_index = jnp.arange(keep_cells, dtype=jnp.int32)
    own_freq = bit_reverse(lon_place, levels)
    source_freq = bit_reverse(shard_index, levels)
    received = send_real(features.reshape(lat_rows, lon_count, stride, channels))
    sectioned_re, sectioned_im = local_sections(received, levels)
    cell_local = lon_place * stride + jnp.arange(stride, dtype=jnp.int32)
    rot_cos, rot_sin = phase_pair(index_outer(source_freq, cell_local), total_lon, -1.0)
    rot_cos = rot_cos[None, :, :, None]
    rot_sin = rot_sin[None, :, :, None]
    section_re = sectioned_re.astype(jnp.float32)
    section_im = sectioned_im.astype(jnp.float32)
    first_re = (section_re * rot_cos - section_im * rot_sin).astype(jnp.bfloat16)
    first_im = (section_re * rot_sin + section_im * rot_cos).astype(jnp.bfloat16)
    first_re, first_im = (
        lax.all_to_all(first_re, "lon", split_axis=1, concat_axis=1, tiled=True),
        lax.all_to_all(first_im, "lon", split_axis=1, concat_axis=1, tiled=True),
    )
    first_re = first_re.reshape(lat_rows, lon_cells, channels)
    first_im = first_im.reshape(lat_rows, lon_cells, channels)
    wave_cos, wave_sin = phase_pair(index_outer(cell_index, keep_index), lon_cells, -1.0)
    lon_re, lon_im = complex_table("rmc,mq->rqc", first_re, first_im, wave_cos, wave_sin)
    col_re, col_im = to_columns(lon_re.astype(jnp.bfloat16), lon_im.astype(jnp.bfloat16))
    row_index = jnp.arange(total_lat, dtype=jnp.int32)
    lat_cos, lat_sin = phase_pair(index_outer(row_index, row_index), total_lat, -1.0)
    spec_re, spec_im = complex_table("rqc,rl->lqc", col_re, col_im, lat_cos, lat_sin)
    spec_re = (spec_re * norm_factor).astype(jnp.bfloat16)
    spec_im = (spec_im * norm_factor).astype(jnp.bfloat16)
    mix_re, mix_im = spectral_mix(spec_re, spec_im, w_first, bias_first, w_second, bias_second)
    back_re, back_im = complex_table("lqc,lr->rqc", mix_re, mix_im, lat_cos, -lat_sin)
    back_re, back_im = to_rows(back_re.astype(jnp.bfloat16), back_im.astype(jnp.bfloat16))
    mode_weight = jnp.where((own_freq == 0) & (keep_index == 0), 1.0, 2.0).astype(jnp.float32)
    inv_cos, inv_sin = phase_pair(index_outer(keep_index, cell_index), lon_cells, 1.0)
    inv_cos = inv_cos * mode_weight[:, None]
    inv_sin = inv_sin * mode_weight[:, None]
    inv_re, inv_im = complex_table("rqc,qm->rmc", back_re, back_im, inv_cos, inv_sin)
    turn_cos, turn_sin = phase_pair(cell_index * own_freq, total_lon, 1.0)
    turn_cos = turn_cos[None, :, None]
    turn_sin = turn_sin[None, :, None]
    lon_back_re = (inv_re * turn_cos - inv_im * turn_sin).astype(jnp.bfloat16)
    lon_back_im = (inv_re * turn_sin + inv_im * turn_cos).astype(jnp.bfloat16)
    lon_back_re = lon_back_re.reshape(lat_rows, lon_count, stride, channels)
    lon_back_im = lon_back_im.reshape(lat_rows, lon_count, stride, channels)
    got_re, got_im = (
        lax.all_to_all(lon_back_re, "lon", split_axis=1, concat_axis=1, tiled=True),
        lax.all_to_all(lon_back_im, "lon", split_axis=1, concat_axis=1, tiled=True),
    )
    back_cos, back_sin = phase_pair(index_outer(source_freq, shard_index), lon_count, 1.0)
    spatial = twin_dot("rxsc,xb->rbsc", got_re, back_cos) - twin_dot(
        "rxsc,xb->rbsc", got_im, back_sin
    )
    filtered = (spatial * norm_factor).astype(jnp.bfloat16)
    filtered = send_real(filtered).reshape(lat_rows, lon_cells, channels)
    return (features.astype(jnp.float32) + filtered.astype(jnp.float32)).astype(jnp.bfloat16)


def lat_tables(total_lat):
    half = total_lat // 2
    row = np.arange(total_lat)
    angle = (np.outer(np.arange(half), row) % total_lat) * (2.0 * np.pi / total_lat)
    sin_part = np.sin(angle)
    sin_part[0] = np.where(row % 2 == 0, 1.0, -1.0)
    forward = np.concatenate([np.cos(angle), sin_part], axis=0)
    return jnp.asarray(forward, jnp.bfloat16), jnp.asarray(forward.T, jnp.bfloat16)


def lon_tables(cell_order, total_lon):
    keep = total_lon // 2
    angle = (np.outer(np.arange(keep), cell_order) % total_lon) * (2.0 * np.pi / total_lon)
    forward = np.concatenate([np.cos(angle), np.sin(angle)], axis=0)
    weight = np.where(np.arange(keep) == 0, 1.0, 2.0)
    weight = np.concatenate([weight, weight])
    backward = (forward * weight[:, None]).T
    return jnp.asarray(forward, jnp.bfloat16), jnp.asarray(backward, jnp.bfloat16)


def dot32(left, right):
    return jnp.dot(left, right, preferred_element_type=jnp.float32)


def lat_forward_kernel(x_ref, table_ref, out_ref, stage):
    sources, cells, rows, channels = x_ref.shape
    half = out_ref.shape[0]
    table = table_ref[...]
    for cell in range(0, cells, 2):
        pair = [x_ref[:, cell + t].reshape(sources * rows, channels) for t in range(2)]
        result = dot32(table, jnp.concatenate(pair, axis=1))
        stage[cell] = result[:, :channels]
        stage[cell + 1] = result[:, channels:]
    for slot in range(half):
        out_ref[slot, :, :channels] = stage[:, slot, :].astype(jnp.bfloat16)
        out_ref[slot, :, channels:] = stage[:, half + slot, :].astype(jnp.bfloat16)


def lat_forward(x, table, cells_per_step):
    sources, cells, rows, channels = x.shape
    total = sources * rows
    return pl.pallas_call(
        lat_forward_kernel,
        grid=(cells // cells_per_step,),
        in_specs=[
            pl.BlockSpec((sources, cells_per_step, rows, channels), lambda i: (0, i, 0, 0)),
            pl.BlockSpec((total, total), lambda i: (0, 0)),
        ],
        out_specs=pl.BlockSpec((total // 2, cells_per_step, 2 * channels), lambda i: (0, i, 0)),
        out_shape=jax.ShapeDtypeStruct((total // 2, cells, 2 * channels), jnp.bfloat16),
        scratch_shapes=[pltpu.VMEM((cells_per_step, total, channels), jnp.float32)],
        compiler_params=pltpu.CompilerParams(vmem_limit_bytes=48 * 2**20),
        cost_estimate=pl.CostEstimate(
            flops=2 * total * total * cells * channels,
            bytes_accessed=4 * total * cells * channels,
            transcendentals=0,
        ),
    )(x, table)


def lat_back_kernel(norm, h_ref, table_ref, out_ref, stage):
    half, cells, width = h_ref.shape
    channels = width // 2
    targets, _, rows, _ = out_ref.shape
    table = table_ref[...]
    stage[:half] = h_ref[:, :, :channels].astype(jnp.float32)
    stage[half:] = h_ref[:, :, channels:].astype(jnp.float32)
    for cell in range(0, cells, 2):
        pair = [stage[:, cell + t, :].astype(jnp.bfloat16) for t in range(2)]
        result = dot32(table, jnp.concatenate(pair, axis=1)) * norm
        for t in range(2):
            part = result[:, t * channels : (t + 1) * channels].astype(jnp.bfloat16)
            out_ref[:, cell + t] = part.reshape(targets, rows, channels)


def lat_back(h, table, targets, cells_per_step, norm):
    half, cells, width = h.shape
    channels = width // 2
    total = 2 * half
    rows = total // targets
    return pl.pallas_call(
        lambda *refs: lat_back_kernel(norm, *refs),
        grid=(cells // cells_per_step,),
        in_specs=[
            pl.BlockSpec((half, cells_per_step, width), lambda i: (0, i, 0)),
            pl.BlockSpec((total, total), lambda i: (0, 0)),
        ],
        out_specs=pl.BlockSpec((targets, cells_per_step, rows, channels), lambda i: (0, i, 0, 0)),
        out_shape=jax.ShapeDtypeStruct((targets, cells, rows, channels), jnp.bfloat16),
        scratch_shapes=[pltpu.VMEM((total, cells_per_step, channels), jnp.float32)],
        compiler_params=pltpu.CompilerParams(vmem_limit_bytes=48 * 2**20),
        cost_estimate=pl.CostEstimate(
            flops=2 * total * total * cells * channels,
            bytes_accessed=4 * total * cells * channels,
            transcendentals=0,
        ),
    )(h, table)


def mix_kernel(norm, place_ref, g_ref, fwd_ref, inv_ref, w1_ref, b1_ref, w2_ref, b2_ref, out_ref):
    sources, _, cells, width = g_ref.shape
    channels = width // 2
    sums = g_ref[:, 0].reshape(sources * cells, width)
    waves = dot32(fwd_ref[...], sums) * norm
    keep = waves.shape[0] // 2
    cc, sc = waves[:keep, :channels], waves[:keep, channels:]
    cs, ss = waves[keep:, :channels], waves[keep:, channels:]
    single = (place_ref[0] + pl.program_id(0)) == 0
    upper = [jnp.where(single, cc, cc - ss), jnp.where(single, -cs, -(cs + sc))]
    lower = [jnp.where(single, sc, cc + ss), jnp.where(single, -ss, sc - cs)]
    modes = jnp.concatenate(
        [jnp.concatenate(upper, axis=1), jnp.concatenate(lower, axis=1)], axis=0
    ).astype(jnp.bfloat16)
    hidden = jnp.maximum(dot32(modes, w1_ref[...]) + b1_ref[...], 0.0).astype(jnp.bfloat16)
    value = dot32(hidden, w2_ref[...]) + b2_ref[...]
    mixed = jnp.maximum(value - shrink_level, 0.0) + jnp.minimum(value + shrink_level, 0.0)
    mixed = mixed.astype(jnp.bfloat16).astype(jnp.float32)
    a, b = mixed[:keep, :channels], mixed[:keep, channels:]
    c, d = mixed[keep:, :channels], mixed[keep:, channels:]
    cos_part = [jnp.where(single, a, a + c), jnp.where(single, c, d - b)]
    sin_part = [jnp.where(single, -b, -(b + d)), jnp.where(single, -d, c - a)]
    coefs = jnp.concatenate(
        [jnp.concatenate(cos_part, axis=1), jnp.concatenate(sin_part, axis=1)], axis=0
    ).astype(jnp.bfloat16)
    back = dot32(inv_ref[...], coefs).astype(jnp.bfloat16)
    out_ref[:, 0] = back.reshape(sources, cells, width)


def spectral_step(g, place, fwd, inv, w1, b1, w2, b2, norm):
    sources, slots, cells, width = g.shape
    total = sources * cells
    block = pl.BlockSpec((sources, 1, cells, width), lambda i, p: (0, i, 0, 0))
    fixed = lambda shape: pl.BlockSpec(shape, lambda i, p: (0,) * len(shape))
    return pl.pallas_call(
        lambda *refs: mix_kernel(norm, *refs),
        grid_spec=pltpu.PrefetchScalarGridSpec(
            num_scalar_prefetch=1,
            grid=(slots,),
            in_specs=[block]
            + [fixed(v.shape) for v in (fwd, inv, w1, b1, w2, b2)],
            out_specs=block,
        ),
        out_shape=jax.ShapeDtypeStruct(g.shape, jnp.bfloat16),
        compiler_params=pltpu.CompilerParams(vmem_limit_bytes=56 * 2**20),
        cost_estimate=pl.CostEstimate(
            flops=slots * width * (4 * total * total + 4 * total * width),
            bytes_accessed=4 * slots * total * width,
            transcendentals=0,
        ),
    )(place, g, fwd, inv, w1, b1, w2, b2)


def complex_weights(weights):
    real, imag = weights[0, 0], weights[1, 0]
    return jnp.concatenate(
        [jnp.concatenate([real, imag], axis=1), jnp.concatenate([-imag, real], axis=1)], axis=0
    )


def lat_first_body(features, w_first, bias_first, w_second, bias_second):
    rows, lon_cells, channels = features.shape
    lat_count, lon_count = lax.axis_size("lat"), lax.axis_size("lon")
    total_lat, total_lon = rows * lat_count, lon_cells * lon_count
    devices = lat_count * lon_count
    cells = lon_cells // lat_count
    slots = total_lat // 2 // devices
    norm = 1.0 / math.sqrt(total_lat * total_lon)
    order = np.arange(total_lon).reshape(lon_count, lat_count, cells).transpose(1, 0, 2).reshape(-1)
    lat_fwd, lat_inv = lat_tables(total_lat)
    lon_fwd, lon_inv = lon_tables(order, total_lon)
    place = (lax.axis_index("lat") * lon_count + lax.axis_index("lon")) * slots
    place = place.astype(jnp.int32).reshape(1)
    w1, w2 = complex_weights(w_first), complex_weights(w_second)
    b1, b2 = bias_first.reshape(1, -1), bias_second.reshape(1, -1)

    sent = features.reshape(rows, lat_count, cells, channels).transpose(1, 2, 0, 3)
    got = lax.all_to_all(sent, "lat", split_axis=0, concat_axis=0, tiled=True)
    sums = lat_forward(got, lat_fwd, 16).reshape(devices, slots, cells, 2 * channels)
    sums = lax.all_to_all(sums, ("lat", "lon"), split_axis=0, concat_axis=0, tiled=True)
    coefs = spectral_step(sums, place, lon_fwd, lon_inv, w1, b1, w2, b2, norm)
    coefs = lax.all_to_all(coefs, ("lat", "lon"), split_axis=0, concat_axis=0, tiled=True)
    coefs = coefs.reshape(devices * slots, cells, 2 * channels)
    filtered = lat_back(coefs, lat_inv, lat_count, 16, norm)
    filtered = lax.all_to_all(filtered, "lat", split_axis=0, concat_axis=0, tiled=True)
    filtered = filtered.transpose(2, 0, 1, 3).reshape(rows, lon_cells, channels)
    return (features.astype(jnp.float32) + filtered.astype(jnp.float32)).astype(jnp.bfloat16)


def body(features, w_first, bias_first, w_second, bias_second):
    rows, lon_cells, channels = features.shape
    lat_count, lon_count = lax.axis_size("lat"), lax.axis_size("lon")
    fits = (
        (rows * lat_count // 2) % (lat_count * lon_count) == 0
        and lon_cells % (16 * lat_count) == 0
        and rows % 16 == 0
        and channels == 128
        and w_first.shape[1] == 1
    )
    chosen = lat_first_body if fits else general_body
    return chosen(features, w_first, bias_first, w_second, bias_second)


def solution(mesh):
    in_specs = (P("lat", "lon", None), P(), P(), P(), P())
    out_specs = P("lat", "lon", None)
    return jax.shard_map(body, mesh=mesh, in_specs=in_specs, out_specs=out_specs, check_vma=False)
```

```python
import math

import jax
import jax.numpy as jnp
import numpy as np
from jax import lax
from jax.experimental import pallas as pl
from jax.experimental.pallas import tpu as pltpu
from jax.sharding import PartitionSpec as P

shrink_level = 0.01


def phase_pair(product, length, sign):
    angle_value = (product % length).astype(jnp.float32) * (sign * 2.0 * math.pi / length)
    return (jnp.cos(angle_value), jnp.sin(angle_value))


def index_outer(left_index, right_index):
    return left_index[:, None] * right_index[None, :]


def twin_dot(pattern, operand, phase_table):
    upper_part = phase_table.astype(jnp.bfloat16)
    lower_part = (phase_table - upper_part.astype(jnp.float32)).astype(jnp.bfloat16)
    return jnp.einsum(
        pattern, operand, upper_part, preferred_element_type=jnp.float32
    ) + jnp.einsum(pattern, operand, lower_part, preferred_element_type=jnp.float32)


def complex_table(pattern, real_part, imag_part, cos_table, sin_table):
    real_out = twin_dot(pattern, real_part, cos_table) - twin_dot(pattern, imag_part, sin_table)
    imag_out = twin_dot(pattern, real_part, sin_table) + twin_dot(pattern, imag_part, cos_table)
    return (real_out, imag_out)


def bit_reverse(number, levels):
    result = jnp.zeros_like(number)
    for bit_level in range(levels):
        result = result + number // 2**bit_level % 2 * 2 ** (levels - 1 - bit_level)
    return result


def local_sections(received, levels):
    full_shape = received.shape
    real_part = received.astype(jnp.float32)
    imag_part = jnp.zeros_like(real_part)
    real_half = received
    imag_half = imag_part.astype(jnp.bfloat16)
    for section_level in range(levels - 1, -1, -1):
        half_span = 2**section_level
        split_shape = (full_shape[0], full_shape[1] // (2 * half_span), 2, half_span) + full_shape[
            2:
        ]
        real_split = real_part.reshape(split_shape)
        imag_split = imag_part.reshape(split_shape)
        tw_cos, tw_sin = phase_pair(jnp.arange(half_span, dtype=jnp.int32), 2 * half_span, -1.0)
        tw_cos = tw_cos[None, None, :, None, None]
        tw_sin = tw_sin[None, None, :, None, None]
        sum_re = real_split[:, :, 0] + real_split[:, :, 1]
        sum_im = imag_split[:, :, 0] + imag_split[:, :, 1]
        diff_re = real_split[:, :, 0] - real_split[:, :, 1]
        diff_im = imag_split[:, :, 0] - imag_split[:, :, 1]
        upper_re = diff_re * tw_cos - diff_im * tw_sin
        upper_im = diff_re * tw_sin + diff_im * tw_cos
        real_half = jnp.stack([sum_re, upper_re], axis=2).reshape(full_shape).astype(jnp.bfloat16)
        imag_half = jnp.stack([sum_im, upper_im], axis=2).reshape(full_shape).astype(jnp.bfloat16)
        real_part = real_half.astype(jnp.float32)
        imag_part = imag_half.astype(jnp.float32)
    return (real_half, imag_half)


def block_product(real_part, imag_part, weights):
    real_out = jnp.einsum(
        "tnj,njk->tnk", real_part, weights[0], preferred_element_type=jnp.float32
    ) - jnp.einsum("tnj,njk->tnk", imag_part, weights[1], preferred_element_type=jnp.float32)
    imag_out = jnp.einsum(
        "tnj,njk->tnk", imag_part, weights[0], preferred_element_type=jnp.float32
    ) + jnp.einsum("tnj,njk->tnk", real_part, weights[1], preferred_element_type=jnp.float32)
    return (real_out, imag_out)


def soft_shrink(values):
    return jnp.sign(values) * jnp.maximum(jnp.abs(values) - shrink_level, 0.0)


def spectral_mix(real_part, imag_part, w_first, bias_first, w_second, bias_second):
    shape_in = real_part.shape
    blocks = w_first.shape[1]
    block_width = w_first.shape[2]
    flat_re = real_part.reshape(-1, blocks, block_width)
    flat_im = imag_part.reshape(-1, blocks, block_width)
    hid_re, hid_im = block_product(flat_re, flat_im, w_first)
    act_re = jax.nn.relu(hid_re + bias_first[0]).astype(jnp.bfloat16)
    act_im = jax.nn.relu(hid_im + bias_first[1]).astype(jnp.bfloat16)
    out_re, out_im = block_product(act_re, act_im, w_second)
    return (
        soft_shrink(out_re + bias_second[0]).astype(jnp.bfloat16).reshape(shape_in),
        soft_shrink(out_im + bias_second[1]).astype(jnp.bfloat16).reshape(shape_in),
    )


def send_real(blocks):
    return lax.all_to_all(blocks, "lon", split_axis=1, concat_axis=1, tiled=True)


def to_columns(real_part, imag_part):
    return (
        lax.all_to_all(real_part, "lat", split_axis=1, concat_axis=0, tiled=True),
        lax.all_to_all(imag_part, "lat", split_axis=1, concat_axis=0, tiled=True),
    )


def to_rows(real_part, imag_part):
    return (
        lax.all_to_all(real_part, "lat", split_axis=0, concat_axis=1, tiled=True),
        lax.all_to_all(imag_part, "lat", split_axis=0, concat_axis=1, tiled=True),
    )


def general_body(features, w_first, bias_first, w_second, bias_second):
    lat_rows, lon_cells, channels = features.shape
    lon_count = lax.axis_size("lon")
    lat_count = lax.axis_size("lat")
    total_lat = lat_rows * lat_count
    total_lon = lon_cells * lon_count
    stride = lon_cells // lon_count
    keep_cells = lon_cells // 2
    norm_factor = 1.0 / math.sqrt(total_lat * total_lon)
    levels = lon_count.bit_length() - 1
    lon_place = lax.axis_index("lon")
    shard_index = jnp.arange(lon_count, dtype=jnp.int32)
    cell_index = jnp.arange(lon_cells, dtype=jnp.int32)
    keep_index = jnp.arange(keep_cells, dtype=jnp.int32)
    own_freq = bit_reverse(lon_place, levels)
    source_freq = bit_reverse(shard_index, levels)
    received = send_real(features.reshape(lat_rows, lon_count, stride, channels))
    sectioned_re, sectioned_im = local_sections(received, levels)
    cell_local = lon_place * stride + jnp.arange(stride, dtype=jnp.int32)
    rot_cos, rot_sin = phase_pair(index_outer(source_freq, cell_local), total_lon, -1.0)
    rot_cos = rot_cos[None, :, :, None]
    rot_sin = rot_sin[None, :, :, None]
    section_re = sectioned_re.astype(jnp.float32)
    section_im = sectioned_im.astype(jnp.float32)
    first_re = (section_re * rot_cos - section_im * rot_sin).astype(jnp.bfloat16)
    first_im = (section_re * rot_sin + section_im * rot_cos).astype(jnp.bfloat16)
    first_re, first_im = (
        lax.all_to_all(first_re, "lon", split_axis=1, concat_axis=1, tiled=True),
        lax.all_to_all(first_im, "lon", split_axis=1, concat_axis=1, tiled=True),
    )
    first_re = first_re.reshape(lat_rows, lon_cells, channels)
    first_im = first_im.reshape(lat_rows, lon_cells, channels)
    wave_cos, wave_sin = phase_pair(index_outer(cell_index, keep_index), lon_cells, -1.0)
    lon_re, lon_im = complex_table("rmc,mq->rqc", first_re, first_im, wave_cos, wave_sin)
    col_re, col_im = to_columns(lon_re.astype(jnp.bfloat16), lon_im.astype(jnp.bfloat16))
    row_index = jnp.arange(total_lat, dtype=jnp.int32)
    lat_cos, lat_sin = phase_pair(index_outer(row_index, row_index), total_lat, -1.0)
    spec_re, spec_im = complex_table("rqc,rl->lqc", col_re, col_im, lat_cos, lat_sin)
    spec_re = (spec_re * norm_factor).astype(jnp.bfloat16)
    spec_im = (spec_im * norm_factor).astype(jnp.bfloat16)
    mix_re, mix_im = spectral_mix(spec_re, spec_im, w_first, bias_first, w_second, bias_second)
    back_re, back_im = complex_table("lqc,lr->rqc", mix_re, mix_im, lat_cos, -lat_sin)
    back_re, back_im = to_rows(back_re.astype(jnp.bfloat16), back_im.astype(jnp.bfloat16))
    mode_weight = jnp.where((own_freq == 0) & (keep_index == 0), 1.0, 2.0).astype(jnp.float32)
    inv_cos, inv_sin = phase_pair(index_outer(keep_index, cell_index), lon_cells, 1.0)
    inv_cos = inv_cos * mode_weight[:, None]
    inv_sin = inv_sin * mode_weight[:, None]
    inv_re, inv_im = complex_table("rqc,qm->rmc", back_re, back_im, inv_cos, inv_sin)
    turn_cos, turn_sin = phase_pair(cell_index * own_freq, total_lon, 1.0)
    turn_cos = turn_cos[None, :, None]
    turn_sin = turn_sin[None, :, None]
    lon_back_re = (inv_re * turn_cos - inv_im * turn_sin).astype(jnp.bfloat16)
    lon_back_im = (inv_re * turn_sin + inv_im * turn_cos).astype(jnp.bfloat16)
    lon_back_re = lon_back_re.reshape(lat_rows, lon_count, stride, channels)
    lon_back_im = lon_back_im.reshape(lat_rows, lon_count, stride, channels)
    got_re, got_im = (
        lax.all_to_all(lon_back_re, "lon", split_axis=1, concat_axis=1, tiled=True),
        lax.all_to_all(lon_back_im, "lon", split_axis=1, concat_axis=1, tiled=True),
    )
    back_cos, back_sin = phase_pair(index_outer(source_freq, shard_index), lon_count, 1.0)
    spatial = twin_dot("rxsc,xb->rbsc", got_re, back_cos) - twin_dot(
        "rxsc,xb->rbsc", got_im, back_sin
    )
    filtered = (spatial * norm_factor).astype(jnp.bfloat16)
    filtered = send_real(filtered).reshape(lat_rows, lon_cells, channels)
    return (features.astype(jnp.float32) + filtered.astype(jnp.float32)).astype(jnp.bfloat16)


def lat_tables(total_lat, lat_count, scale):
    half = total_lat // 2
    row = np.arange(total_lat)
    angle = (np.outer(np.arange(half), row) % total_lat) * (2.0 * np.pi / total_lat)
    sin_part = np.sin(angle)
    sin_part[0] = np.where(row % 2 == 0, 1.0, -1.0)
    forward = np.concatenate([np.cos(angle), sin_part], axis=0)
    forward = forward.reshape(total_lat, lat_count, total_lat // lat_count)
    places = np.arange(lat_count)
    tables = [forward[:, p ^ places].reshape(total_lat, total_lat) for p in range(lat_count)]
    tables = np.stack(tables)
    return (
        jnp.asarray(tables, jnp.bfloat16),
        jnp.asarray(tables.transpose(0, 2, 1) * scale, jnp.bfloat16),
    )


def lon_tables(cell_order, total_lon, scale):
    keep = total_lon // 2
    angle = (np.outer(np.arange(keep), cell_order) % total_lon) * (2.0 * np.pi / total_lon)
    forward = np.concatenate([np.cos(angle), -np.sin(angle)], axis=0)
    weight = np.where(np.arange(keep) == 0, 1.0, 2.0)
    weight = np.concatenate([weight, weight])
    backward = (forward * weight[:, None]).T
    return jnp.asarray(forward * scale, jnp.bfloat16), jnp.asarray(backward, jnp.bfloat16)


def dot32(left, right):
    return jnp.dot(left, right, preferred_element_type=jnp.float32)


def turn(values):
    return jnp.transpose(values, (1, 0, 2))


def call(kernel, place, args, in_specs, out_specs, out_shape, grid, mib=24, alias=None):
    return pl.pallas_call(
        kernel,
        grid_spec=pltpu.PrefetchScalarGridSpec(
            num_scalar_prefetch=1, grid=grid, in_specs=in_specs, out_specs=out_specs
        ),
        out_shape=out_shape,
        input_output_aliases=alias or {},
        compiler_params=pltpu.CompilerParams(vmem_limit_bytes=mib * 2**20),
        cost_estimate=pl.CostEstimate(flops=1, bytes_accessed=2**20, transcendentals=0),
    )(place, *args)


def own_block(tile, chips, cells, start, flip):
    return pl.BlockSpec(
        (tile, chips, 1, cells, 128), lambda i, p: (i, 0, (p[0] % 2) ^ flip, start // cells, 0)
    )


def split_rows(features, twin, place, start, cells, steps=4):
    rows, chips, _, _, channels = features.shape
    tile = rows // steps

    def kernel(place_ref, x_ref, twin_ref, *outs):
        chip = place_ref[0] // 2
        for d in range(chips):
            outs[d][:, 0] = turn(x_ref[:, chip ^ d, 0])
            outs[d][:, 1] = turn(twin_ref[:, chip ^ d])

    out = pl.BlockSpec((cells, 2, tile, channels), lambda i, p: (0, 0, i, 0))
    return call(
        kernel,
        place,
        [features, twin],
        [
            own_block(tile, chips, cells, start, 0),
            pl.BlockSpec((tile, chips, cells, channels), lambda i, p: (i, 0, 0, 0)),
        ],
        [out] * chips,
        [jax.ShapeDtypeStruct((cells, 2, rows, channels), jnp.bfloat16)] * chips,
        (steps,),
    )


def join_own(features, parts, place, start, partial, steps=4):
    rows, chips, _, _, channels = features.shape
    cells = parts[0].shape[0]
    tile = rows // steps

    def kernel(place_ref, x_ref, *refs):
        out_ref, twin_ref = refs[-2:]
        chip = place_ref[0] // 2
        for d in range(chips):
            added = x_ref[:, chip ^ d, 0].astype(jnp.float32) + turn(refs[d][:, 0]).astype(jnp.float32)
            out_ref[:, chip ^ d, 0] = added.astype(jnp.bfloat16)
            twin_ref[:, chip ^ d] = turn(refs[d][:, 1])

    block = own_block(tile, chips, cells, start, 0)
    part = pl.BlockSpec((cells, 2, tile, channels), lambda i, p: (0, 0, i, 0))
    args, specs, alias = [features, *parts], [block] + [part] * chips, None
    if partial is not None:
        args, specs, alias = args + [partial], specs + [pl.BlockSpec(memory_space=pl.ANY)], {len(args) + 1: 0}
    return call(
        kernel,
        place,
        args,
        specs,
        [block, pl.BlockSpec((tile, chips, cells, channels), lambda i, p: (i, 0, 0, 0))],
        [
            jax.ShapeDtypeStruct(features.shape, jnp.bfloat16),
            jax.ShapeDtypeStruct((rows, chips, cells, channels), jnp.bfloat16),
        ],
        (steps,),
        alias=alias,
    )


def join_twin(features, twin, place, start, partial, steps=2):
    rows, chips, cells, channels = twin.shape
    tile = rows // steps

    def kernel(place_ref, x_ref, twin_ref, partial_ref, out_ref):
        added = x_ref[:, :, 0].astype(jnp.float32) + twin_ref[...].astype(jnp.float32)
        out_ref[:, :, 0] = added.astype(jnp.bfloat16)

    block = own_block(tile, chips, cells, start, 1)
    return call(
        kernel,
        place,
        [features, twin, partial],
        [
            block,
            pl.BlockSpec((tile, chips, cells, channels), lambda i, p: (i, 0, 0, 0)),
            pl.BlockSpec(memory_space=pl.ANY),
        ],
        block,
        jax.ShapeDtypeStruct(features.shape, jnp.bfloat16),
        (steps,),
        alias={3: 0},
    )


def lat_forward(parts, table, place, step_cells=8):
    cells, rows, channels = parts[0].shape
    count = len(parts)
    total = rows * count
    half = total // 2

    def kernel(place_ref, *refs):
        xs, (table_ref, out_ref) = refs[:count], refs[count:]
        sums = []
        for cell in range(0, step_cells, 2):
            pair = [jnp.concatenate([x[cell + t] for x in xs], axis=0) for t in range(2)]
            result = dot32(table_ref[0], jnp.concatenate(pair, axis=1)).astype(jnp.bfloat16)
            sums += [result[:, :channels], result[:, channels:]]
        for part in range(2):
            lines = jnp.stack([v[part * half : (part + 1) * half] for v in sums], axis=0)
            out_ref[:, :, part * channels : (part + 1) * channels] = turn(lines)

    return call(
        kernel,
        place,
        [*parts, table],
        [pl.BlockSpec((step_cells, rows, channels), lambda i, p: (i, 0, 0))] * count
        + [pl.BlockSpec((1, total, total), lambda i, p: (p[0], 0, 0))],
        pl.BlockSpec((half, step_cells, 2 * channels), lambda i, p: (0, i, 0)),
        jax.ShapeDtypeStruct((half, cells, 2 * channels), jnp.bfloat16),
        (cells // step_cells,),
    )


def lat_back(h, table, place, chips, step_cells=8):
    half, cells, width = h.shape
    channels = width // 2
    total = 2 * half
    rows = total // chips // 2

    def kernel(place_ref, h_ref, table_ref, *outs):
        lines = [turn(h_ref[:, :, part * channels : (part + 1) * channels]) for part in range(2)]
        for cell in range(0, step_cells, 2):
            pair = [jnp.concatenate([v[cell + t] for v in lines], axis=0) for t in range(2)]
            result = dot32(table_ref[0], jnp.concatenate(pair, axis=1)).astype(jnp.bfloat16)
            for t in range(2):
                part = result[:, t * channels : (t + 1) * channels].reshape(chips, 2, rows, channels)
                for d in range(chips):
                    outs[d][cell + t] = part[d]

    return call(
        kernel,
        place,
        [h, table],
        [
            pl.BlockSpec((half, step_cells, width), lambda i, p: (0, i, 0)),
            pl.BlockSpec((1, total, total), lambda i, p: (p[0], 0, 0)),
        ],
        [pl.BlockSpec((step_cells, 2, rows, channels), lambda i, p: (i, 0, 0, 0))] * chips,
        [jax.ShapeDtypeStruct((cells, 2, rows, channels), jnp.bfloat16)] * chips,
        (cells // step_cells,),
    )


def spectral_step(chunks, place, fwd, inv, w1, b1, w2, b2, together=2):
    count = len(chunks)
    sources, slots, _, width = chunks[0].shape
    channels = width // 2
    sizes = [sources * g.shape[2] for g in chunks]
    total = sum(sizes)
    keep = total // 2

    def kernel(place_ref, *refs):
        gs, (fwd_ref, inv_ref, w1_ref, b1_ref, w2_ref, b2_ref) = refs[:count], refs[count : count + 6]
        outs = refs[count + 6 :]

        def waves(u):
            sums = jnp.concatenate([g[:, u].reshape(size, width) for g, size in zip(gs, sizes)], axis=0)
            return dot32(fwd_ref[...], sums)

        def mix(u, both):
            cc, sc = both[:keep, :channels], both[:keep, channels:]
            cs, ss = both[keep:, :channels], both[keep:, channels:]
            single = (place_ref[1] + pl.program_id(0) * together + u) == 0
            upper = [jnp.where(single, cc, cc + ss), jnp.where(single, cs, cs - sc)]
            lower = [jnp.where(single, sc, cc - ss), jnp.where(single, ss, cs + sc)]
            modes = [jnp.concatenate([v.astype(jnp.bfloat16) for v in part], axis=1) for part in (upper, lower)]
            modes = jnp.concatenate(modes, axis=0)
            hidden = jnp.maximum((dot32(modes, w1_ref[...]) + b1_ref[...]).astype(jnp.bfloat16), 0)
            value = dot32(hidden, w2_ref[...]) + b2_ref[...]
            mixed = value - jnp.clip(value, -shrink_level, shrink_level)
            a, b = mixed[:keep, :channels], mixed[:keep, channels:]
            c, d = mixed[keep:, :channels], mixed[keep:, channels:]
            cos_part = [jnp.where(single, a, a + c), jnp.where(single, c, d - b)]
            sin_part = [jnp.where(single, b, b + d), jnp.where(single, d, a - c)]
            coefs = [jnp.concatenate([v.astype(jnp.bfloat16) for v in part], axis=1) for part in (cos_part, sin_part)]
            return jnp.concatenate(coefs, axis=0)

        def back(u, coefs):
            lines = dot32(inv_ref[...], coefs).astype(jnp.bfloat16)
            first = 0
            for out_ref, size in zip(outs, sizes):
                out_ref[:, u] = lines[first : first + size].reshape(sources, size // sources, width)
                first += size

        both = [waves(u) for u in range(together)]
        coefs = [mix(u, both[u]) for u in range(together)]
        for u in range(together):
            back(u, coefs[u])

    def block(g):
        return pl.BlockSpec((sources, together) + g.shape[2:], lambda i, p: (0, i, 0, 0))

    tables = [fwd, inv, w1, b1, w2, b2]
    return call(
        kernel,
        place,
        [*chunks, *tables],
        [block(g) for g in chunks] + [pl.BlockSpec(v.shape, lambda i, p: (0, 0)) for v in tables],
        [block(g) for g in chunks],
        [jax.ShapeDtypeStruct(g.shape, jnp.bfloat16) for g in chunks],
        (slots // together,),
        mib=48,
    )


def complex_weights(weights):
    real, imag = weights[0, 0], weights[1, 0]
    return jnp.concatenate(
        [jnp.concatenate([real, imag], axis=1), jnp.concatenate([-imag, real], axis=1)], axis=0
    )


def swap(part, axis, bits):
    return lax.ppermute(part, axis, [(j, j ^ bits) for j in range(lax.axis_size(axis))])


def swap_chips(parts):
    return [parts[0]] + [swap(parts[d], "lat", 2 * d) for d in range(1, len(parts))]


def swap_all(parts):
    return lax.all_to_all(parts, ("lat", "lon"), split_axis=0, concat_axis=0, tiled=True)


def chunk_sizes(cells):
    return [cells // 2, cells // 2]


def lat_first_body(features, w_first, bias_first, w_second, bias_second):
    rows, lon_cells, channels = features.shape
    lat_count, lon_count = lax.axis_size("lat"), lax.axis_size("lon")
    total_lat, total_lon = rows * lat_count, lon_cells * lon_count
    devices, chips = lat_count * lon_count, lat_count // 2
    block_cells = lon_cells // lat_count
    slots = total_lat // 2 // devices
    norm = 1.0 / math.sqrt(total_lat * total_lon)
    sizes = chunk_sizes(block_cells)
    count = len(sizes)
    starts = [sum(sizes[:i]) for i in range(count)]
    cell_index = np.arange(total_lon).reshape(lon_count, lat_count, block_cells).transpose(1, 0, 2)
    order = [cell_index[..., s : s + n].reshape(-1) for s, n in zip(starts, sizes)]
    lat_fwd, lat_inv = lat_tables(total_lat, lat_count, norm)
    lon_fwd, lon_inv = lon_tables(np.concatenate(order), total_lon, norm)
    lat_place = lax.axis_index("lat")
    first_slot = (lat_place * lon_count + lax.axis_index("lon")) * slots
    place = jnp.stack([lat_place, first_slot]).astype(jnp.int32)
    w1, w2 = complex_weights(w_first), complex_weights(w_second)
    b1, b2 = bias_first.reshape(1, -1), bias_second.reshape(1, -1)
    tie = lax.optimization_barrier
    field = features.reshape(rows, chips, 2, block_cells, channels)

    def prepare(i):
        for_twin = lax.dynamic_slice(
            field, (0, 0, 1 - lat_place % 2, starts[i], 0), (rows, chips, 1, sizes[i], channels)
        )
        twin = swap(for_twin.reshape(rows, chips, sizes[i], channels), "lat", 1)
        return split_rows(field, twin, place, starts[i], sizes[i])

    sums, sent = [], prepare(0)
    for i, size in enumerate(sizes):
        parts = swap_chips([v.reshape(size, 2 * rows, channels) for v in sent])
        if i + 1 < count:
            parts, sent = tie((parts, prepare(i + 1)))
        part = lat_forward(parts, lat_fwd, place)
        sums.append(swap_all(part.reshape(devices, slots, size, 2 * channels)))

    coefs = spectral_step(sums, place, lon_fwd, lon_inv, w1, b1, w2, b2)

    def finish(i, parts, result):
        result, for_twin = join_own(field, parts, place, starts[i], result)
        return join_twin(field, swap(for_twin, "lat", 1), place, starts[i], result)

    result, parts = None, None
    for i in reversed(range(count)):
        part = swap_all(coefs[i]).reshape(devices * slots, sizes[i], 2 * channels)
        if parts is not None:
            part, parts = tie((part, parts))
        back = lat_back(part, lat_inv, place, chips)
        if parts is not None:
            result = finish(i + 1, parts, result)
        parts = swap_chips(back)
    result = finish(0, parts, result)
    return result.reshape(features.shape)


def body(features, w_first, bias_first, w_second, bias_second):
    rows, lon_cells, channels = features.shape
    lat_count, lon_count = lax.axis_size("lat"), lax.axis_size("lon")
    fits = (
        (rows * lat_count // 2) % (lat_count * lon_count) == 0
        and lat_count & (lat_count - 1) == 0
        and lat_count > 1
        and lon_cells % (32 * lat_count) == 0
        and rows % 64 == 0
        and channels == 128
        and w_first.shape[1] == 1
    )
    chosen = lat_first_body if fits else general_body
    return chosen(features, w_first, bias_first, w_second, bias_second)


def solution(mesh):
    in_specs = (P("lat", "lon", None), P(), P(), P(), P())
    out_specs = P("lat", "lon", None)
    return jax.shard_map(body, mesh=mesh, in_specs=in_specs, out_specs=out_specs, check_vma=False)
```

```python
import math

import jax
import jax.numpy as jnp
import numpy as np
from jax import lax
from jax.experimental import pallas as pl
from jax.experimental.pallas import tpu as pltpu
from jax.sharding import PartitionSpec as P

shrink_level = 0.01


def phase_pair(product, length, sign):
    angle_value = (product % length).astype(jnp.float32) * (sign * 2.0 * math.pi / length)
    return (jnp.cos(angle_value), jnp.sin(angle_value))


def index_outer(left_index, right_index):
    return left_index[:, None] * right_index[None, :]


def twin_dot(pattern, operand, phase_table):
    upper_part = phase_table.astype(jnp.bfloat16)
    lower_part = (phase_table - upper_part.astype(jnp.float32)).astype(jnp.bfloat16)
    return jnp.einsum(
        pattern, operand, upper_part, preferred_element_type=jnp.float32
    ) + jnp.einsum(pattern, operand, lower_part, preferred_element_type=jnp.float32)


def complex_table(pattern, real_part, imag_part, cos_table, sin_table):
    real_out = twin_dot(pattern, real_part, cos_table) - twin_dot(pattern, imag_part, sin_table)
    imag_out = twin_dot(pattern, real_part, sin_table) + twin_dot(pattern, imag_part, cos_table)
    return (real_out, imag_out)


def bit_reverse(number, levels):
    result = jnp.zeros_like(number)
    for bit_level in range(levels):
        result = result + number // 2**bit_level % 2 * 2 ** (levels - 1 - bit_level)
    return result


def local_sections(received, levels):
    full_shape = received.shape
    real_part = received.astype(jnp.float32)
    imag_part = jnp.zeros_like(real_part)
    real_half = received
    imag_half = imag_part.astype(jnp.bfloat16)
    for section_level in range(levels - 1, -1, -1):
        half_span = 2**section_level
        split_shape = (full_shape[0], full_shape[1] // (2 * half_span), 2, half_span) + full_shape[
            2:
        ]
        real_split = real_part.reshape(split_shape)
        imag_split = imag_part.reshape(split_shape)
        tw_cos, tw_sin = phase_pair(jnp.arange(half_span, dtype=jnp.int32), 2 * half_span, -1.0)
        tw_cos = tw_cos[None, None, :, None, None]
        tw_sin = tw_sin[None, None, :, None, None]
        sum_re = real_split[:, :, 0] + real_split[:, :, 1]
        sum_im = imag_split[:, :, 0] + imag_split[:, :, 1]
        diff_re = real_split[:, :, 0] - real_split[:, :, 1]
        diff_im = imag_split[:, :, 0] - imag_split[:, :, 1]
        upper_re = diff_re * tw_cos - diff_im * tw_sin
        upper_im = diff_re * tw_sin + diff_im * tw_cos
        real_half = jnp.stack([sum_re, upper_re], axis=2).reshape(full_shape).astype(jnp.bfloat16)
        imag_half = jnp.stack([sum_im, upper_im], axis=2).reshape(full_shape).astype(jnp.bfloat16)
        real_part = real_half.astype(jnp.float32)
        imag_part = imag_half.astype(jnp.float32)
    return (real_half, imag_half)


def block_product(real_part, imag_part, weights):
    real_out = jnp.einsum(
        "tnj,njk->tnk", real_part, weights[0], preferred_element_type=jnp.float32
    ) - jnp.einsum("tnj,njk->tnk", imag_part, weights[1], preferred_element_type=jnp.float32)
    imag_out = jnp.einsum(
        "tnj,njk->tnk", imag_part, weights[0], preferred_element_type=jnp.float32
    ) + jnp.einsum("tnj,njk->tnk", real_part, weights[1], preferred_element_type=jnp.float32)
    return (real_out, imag_out)


def soft_shrink(values):
    return jnp.sign(values) * jnp.maximum(jnp.abs(values) - shrink_level, 0.0)


def spectral_mix(real_part, imag_part, w_first, bias_first, w_second, bias_second):
    shape_in = real_part.shape
    blocks = w_first.shape[1]
    block_width = w_first.shape[2]
    flat_re = real_part.reshape(-1, blocks, block_width)
    flat_im = imag_part.reshape(-1, blocks, block_width)
    hid_re, hid_im = block_product(flat_re, flat_im, w_first)
    act_re = jax.nn.relu(hid_re + bias_first[0]).astype(jnp.bfloat16)
    act_im = jax.nn.relu(hid_im + bias_first[1]).astype(jnp.bfloat16)
    out_re, out_im = block_product(act_re, act_im, w_second)
    return (
        soft_shrink(out_re + bias_second[0]).astype(jnp.bfloat16).reshape(shape_in),
        soft_shrink(out_im + bias_second[1]).astype(jnp.bfloat16).reshape(shape_in),
    )


def send_real(blocks):
    return lax.all_to_all(blocks, "lon", split_axis=1, concat_axis=1, tiled=True)


def to_columns(real_part, imag_part):
    return (
        lax.all_to_all(real_part, "lat", split_axis=1, concat_axis=0, tiled=True),
        lax.all_to_all(imag_part, "lat", split_axis=1, concat_axis=0, tiled=True),
    )


def to_rows(real_part, imag_part):
    return (
        lax.all_to_all(real_part, "lat", split_axis=0, concat_axis=1, tiled=True),
        lax.all_to_all(imag_part, "lat", split_axis=0, concat_axis=1, tiled=True),
    )


def general_body(features, w_first, bias_first, w_second, bias_second):
    lat_rows, lon_cells, channels = features.shape
    lon_count = lax.axis_size("lon")
    lat_count = lax.axis_size("lat")
    total_lat = lat_rows * lat_count
    total_lon = lon_cells * lon_count
    stride = lon_cells // lon_count
    keep_cells = lon_cells // 2
    norm_factor = 1.0 / math.sqrt(total_lat * total_lon)
    levels = lon_count.bit_length() - 1
    lon_place = lax.axis_index("lon")
    shard_index = jnp.arange(lon_count, dtype=jnp.int32)
    cell_index = jnp.arange(lon_cells, dtype=jnp.int32)
    keep_index = jnp.arange(keep_cells, dtype=jnp.int32)
    own_freq = bit_reverse(lon_place, levels)
    source_freq = bit_reverse(shard_index, levels)
    received = send_real(features.reshape(lat_rows, lon_count, stride, channels))
    sectioned_re, sectioned_im = local_sections(received, levels)
    cell_local = lon_place * stride + jnp.arange(stride, dtype=jnp.int32)
    rot_cos, rot_sin = phase_pair(index_outer(source_freq, cell_local), total_lon, -1.0)
    rot_cos = rot_cos[None, :, :, None]
    rot_sin = rot_sin[None, :, :, None]
    section_re = sectioned_re.astype(jnp.float32)
    section_im = sectioned_im.astype(jnp.float32)
    first_re = (section_re * rot_cos - section_im * rot_sin).astype(jnp.bfloat16)
    first_im = (section_re * rot_sin + section_im * rot_cos).astype(jnp.bfloat16)
    first_re, first_im = (
        lax.all_to_all(first_re, "lon", split_axis=1, concat_axis=1, tiled=True),
        lax.all_to_all(first_im, "lon", split_axis=1, concat_axis=1, tiled=True),
    )
    first_re = first_re.reshape(lat_rows, lon_cells, channels)
    first_im = first_im.reshape(lat_rows, lon_cells, channels)
    wave_cos, wave_sin = phase_pair(index_outer(cell_index, keep_index), lon_cells, -1.0)
    lon_re, lon_im = complex_table("rmc,mq->rqc", first_re, first_im, wave_cos, wave_sin)
    col_re, col_im = to_columns(lon_re.astype(jnp.bfloat16), lon_im.astype(jnp.bfloat16))
    row_index = jnp.arange(total_lat, dtype=jnp.int32)
    lat_cos, lat_sin = phase_pair(index_outer(row_index, row_index), total_lat, -1.0)
    spec_re, spec_im = complex_table("rqc,rl->lqc", col_re, col_im, lat_cos, lat_sin)
    spec_re = (spec_re * norm_factor).astype(jnp.bfloat16)
    spec_im = (spec_im * norm_factor).astype(jnp.bfloat16)
    mix_re, mix_im = spectral_mix(spec_re, spec_im, w_first, bias_first, w_second, bias_second)
    back_re, back_im = complex_table("lqc,lr->rqc", mix_re, mix_im, lat_cos, -lat_sin)
    back_re, back_im = to_rows(back_re.astype(jnp.bfloat16), back_im.astype(jnp.bfloat16))
    mode_weight = jnp.where((own_freq == 0) & (keep_index == 0), 1.0, 2.0).astype(jnp.float32)
    inv_cos, inv_sin = phase_pair(index_outer(keep_index, cell_index), lon_cells, 1.0)
    inv_cos = inv_cos * mode_weight[:, None]
    inv_sin = inv_sin * mode_weight[:, None]
    inv_re, inv_im = complex_table("rqc,qm->rmc", back_re, back_im, inv_cos, inv_sin)
    turn_cos, turn_sin = phase_pair(cell_index * own_freq, total_lon, 1.0)
    turn_cos = turn_cos[None, :, None]
    turn_sin = turn_sin[None, :, None]
    lon_back_re = (inv_re * turn_cos - inv_im * turn_sin).astype(jnp.bfloat16)
    lon_back_im = (inv_re * turn_sin + inv_im * turn_cos).astype(jnp.bfloat16)
    lon_back_re = lon_back_re.reshape(lat_rows, lon_count, stride, channels)
    lon_back_im = lon_back_im.reshape(lat_rows, lon_count, stride, channels)
    got_re, got_im = (
        lax.all_to_all(lon_back_re, "lon", split_axis=1, concat_axis=1, tiled=True),
        lax.all_to_all(lon_back_im, "lon", split_axis=1, concat_axis=1, tiled=True),
    )
    back_cos, back_sin = phase_pair(index_outer(source_freq, shard_index), lon_count, 1.0)
    spatial = twin_dot("rxsc,xb->rbsc", got_re, back_cos) - twin_dot(
        "rxsc,xb->rbsc", got_im, back_sin
    )
    filtered = (spatial * norm_factor).astype(jnp.bfloat16)
    filtered = send_real(filtered).reshape(lat_rows, lon_cells, channels)
    return (features.astype(jnp.float32) + filtered.astype(jnp.float32)).astype(jnp.bfloat16)


def lat_tables(total_lat, lat_count, scale):
    half = total_lat // 2
    row = np.arange(total_lat)
    angle = (np.outer(np.arange(half), row) % total_lat) * (2.0 * np.pi / total_lat)
    sin_part = np.sin(angle)
    sin_part[0] = np.where(row % 2 == 0, 1.0, -1.0)
    forward = np.concatenate([np.cos(angle), sin_part], axis=0)
    forward = forward.reshape(total_lat, lat_count, total_lat // lat_count)
    places = np.arange(lat_count)
    tables = [forward[:, p ^ places].reshape(total_lat, total_lat) for p in range(lat_count)]
    tables = np.stack(tables)
    back = tables.transpose(0, 2, 1) * scale
    return jnp.asarray(tables, jnp.bfloat16), jnp.asarray(back, jnp.bfloat16)


def lon_tables(cell_order, total_lon, scale):
    keep = total_lon // 2
    angle = (np.outer(np.arange(keep), cell_order) % total_lon) * (2.0 * np.pi / total_lon)
    forward = np.concatenate([np.cos(angle), -np.sin(angle)], axis=0)
    weight = np.where(np.arange(keep) == 0, 1.0, 2.0)
    weight = np.concatenate([weight, weight])
    backward = (forward * weight[:, None]).T
    return jnp.asarray(forward * scale, jnp.bfloat16), jnp.asarray(backward, jnp.bfloat16)


def dot32(left, right):
    return jnp.dot(left, right, preferred_element_type=jnp.float32)


def turn(values):
    return jnp.transpose(values, (1, 0, 2))


def call(kernel, place, args, in_specs, out_specs, out_shape, grid, mib=24, alias=None):
    return pl.pallas_call(
        kernel,
        grid_spec=pltpu.PrefetchScalarGridSpec(
            num_scalar_prefetch=1, grid=grid, in_specs=in_specs, out_specs=out_specs
        ),
        out_shape=out_shape,
        input_output_aliases=alias or {},
        compiler_params=pltpu.CompilerParams(vmem_limit_bytes=mib * 2**20),
        cost_estimate=pl.CostEstimate(flops=1, bytes_accessed=2**20, transcendentals=0),
    )(place, *args)


def own_block(tile, chips, cells, start, flip):
    return pl.BlockSpec(
        (tile, chips, 1, cells, 128), lambda i, p: (i, 0, (p[0] % 2) ^ flip, start // cells, 0)
    )


def split_rows(features, twin, place, start, cells, steps=4):
    rows, chips, _, _, channels = features.shape
    tile = rows // steps

    def kernel(place_ref, x_ref, twin_ref, *outs):
        chip = place_ref[0] // 2
        for d in range(chips):
            outs[d][0] = turn(x_ref[:, chip ^ d, 0])
            outs[d][1] = turn(twin_ref[:, chip ^ d])

    out = pl.BlockSpec((2, cells, tile, channels), lambda i, p: (0, 0, i, 0))
    return call(
        kernel,
        place,
        [features, twin],
        [
            own_block(tile, chips, cells, start, 0),
            pl.BlockSpec((tile, chips, cells, channels), lambda i, p: (i, 0, 0, 0)),
        ],
        [out] * chips,
        [jax.ShapeDtypeStruct((2, cells, rows, channels), jnp.bfloat16)] * chips,
        (steps,),
    )


def join_own(features, parts, place, start, partial, steps=4):
    rows, chips, _, _, channels = features.shape
    cells = parts[0].shape[1]
    tile = rows // steps

    def kernel(place_ref, x_ref, *refs):
        out_ref, twin_ref = refs[-2:]
        chip = place_ref[0] // 2
        for d in range(chips):
            added = x_ref[:, chip ^ d, 0].astype(jnp.float32) + turn(refs[d][0]).astype(jnp.float32)
            out_ref[:, chip ^ d, 0] = added.astype(jnp.bfloat16)
            twin_ref[:, chip ^ d] = turn(refs[d][1])

    block = own_block(tile, chips, cells, start, 0)
    part = pl.BlockSpec((2, cells, tile, channels), lambda i, p: (0, 0, i, 0))
    args, specs, alias = [features, *parts], [block] + [part] * chips, None
    if partial is not None:
        args, specs, alias = args + [partial], specs + [pl.BlockSpec(memory_space=pl.ANY)], {len(args) + 1: 0}
    return call(
        kernel,
        place,
        args,
        specs,
        [block, pl.BlockSpec((tile, chips, cells, channels), lambda i, p: (i, 0, 0, 0))],
        [
            jax.ShapeDtypeStruct(features.shape, jnp.bfloat16),
            jax.ShapeDtypeStruct((rows, chips, cells, channels), jnp.bfloat16),
        ],
        (steps,),
        alias=alias,
    )


def join_twin(features, twin, place, start, partial, steps=2):
    rows, chips, cells, channels = twin.shape
    tile = rows // steps

    def kernel(place_ref, x_ref, twin_ref, partial_ref, out_ref):
        added = x_ref[:, :, 0].astype(jnp.float32) + twin_ref[...].astype(jnp.float32)
        out_ref[:, :, 0] = added.astype(jnp.bfloat16)

    block = own_block(tile, chips, cells, start, 1)
    return call(
        kernel,
        place,
        [features, twin, partial],
        [
            block,
            pl.BlockSpec((tile, chips, cells, channels), lambda i, p: (i, 0, 0, 0)),
            pl.BlockSpec(memory_space=pl.ANY),
        ],
        block,
        jax.ShapeDtypeStruct(features.shape, jnp.bfloat16),
        (steps,),
        alias={3: 0},
    )


def split_all(features, place, start, cells, steps=4):
    rows, chips, cores, _, channels = features.shape
    tile = rows // steps

    def kernel(place_ref, x_ref, out_ref):
        for j in range(chips * cores):
            out_ref[j] = turn(x_ref[:, j // cores, j % cores])

    return call(
        kernel,
        place,
        [features],
        [pl.BlockSpec((tile, chips, cores, cells, channels), lambda i, p: (i, 0, 0, start // cells, 0))],
        pl.BlockSpec((chips * cores, cells, tile, channels), lambda i, p: (0, 0, i, 0)),
        jax.ShapeDtypeStruct((chips * cores, cells, rows, channels), jnp.bfloat16),
        (steps,),
    )


def join_all(features, part, place, start, partial, steps=4):
    rows, chips, cores, _, channels = features.shape
    cells = part.shape[1]
    tile = rows // steps

    def kernel(place_ref, x_ref, part_ref, partial_ref, out_ref):
        for j in range(chips * cores):
            at = (slice(None), j // cores, j % cores)
            added = x_ref[at].astype(jnp.float32) + turn(part_ref[j]).astype(jnp.float32)
            out_ref[at] = added.astype(jnp.bfloat16)

    block = pl.BlockSpec(
        (tile, chips, cores, cells, channels), lambda i, p: (i, 0, 0, start // cells, 0)
    )
    return call(
        kernel,
        place,
        [features, part, partial],
        [
            block,
            pl.BlockSpec((chips * cores, cells, tile, channels), lambda i, p: (0, 0, i, 0)),
            pl.BlockSpec(memory_space=pl.ANY),
        ],
        block,
        jax.ShapeDtypeStruct(features.shape, jnp.bfloat16),
        (steps,),
        alias={3: 0},
    )


def lat_forward(parts, table, place, step_cells=8):
    sources, cells, rows, channels = parts[0].shape
    count = len(parts)
    total = sources * rows * count
    half = total // 2

    def kernel(place_ref, *refs):
        xs, (table_ref, out_ref) = refs[:count], refs[count:]
        sums = []
        for cell in range(0, step_cells, 2):
            pair = [
                jnp.concatenate([x[j, cell + t] for x in xs for j in range(sources)], axis=0)
                for t in range(2)
            ]
            result = dot32(table_ref[...], jnp.concatenate(pair, axis=1)).astype(jnp.bfloat16)
            sums += [result[:, :channels], result[:, channels:]]
        for part in range(2):
            lines = jnp.stack([v[part * half : (part + 1) * half] for v in sums], axis=0)
            out_ref[:, :, part * channels : (part + 1) * channels] = turn(lines)

    return call(
        kernel,
        place,
        [*parts, table],
        [pl.BlockSpec((sources, step_cells, rows, channels), lambda i, p: (0, i, 0, 0))] * count
        + [pl.BlockSpec((total, total), lambda i, p: (0, 0))],
        pl.BlockSpec((half, step_cells, 2 * channels), lambda i, p: (0, i, 0)),
        jax.ShapeDtypeStruct((half, cells, 2 * channels), jnp.bfloat16),
        (cells // step_cells,),
    )


def lat_back(h, table, place, groups, count, step_cells=8):
    half, cells, width = h.shape
    channels = width // 2
    total = 2 * half
    rows = total // groups // count

    def kernel(place_ref, h_ref, table_ref, *outs):
        lines = [turn(h_ref[:, :, part * channels : (part + 1) * channels]) for part in range(2)]
        for cell in range(0, step_cells, 2):
            pair = [jnp.concatenate([v[cell + t] for v in lines], axis=0) for t in range(2)]
            result = dot32(table_ref[...], jnp.concatenate(pair, axis=1)).astype(jnp.bfloat16)
            for t in range(2):
                part = result[:, t * channels : (t + 1) * channels].reshape(count, groups, rows, channels)
                for d in range(count):
                    outs[d][:, cell + t] = part[d]

    return call(
        kernel,
        place,
        [h, table],
        [
            pl.BlockSpec((half, step_cells, width), lambda i, p: (0, i, 0)),
            pl.BlockSpec((total, total), lambda i, p: (0, 0)),
        ],
        [pl.BlockSpec((groups, step_cells, rows, channels), lambda i, p: (0, i, 0, 0))] * count,
        [jax.ShapeDtypeStruct((groups, cells, rows, channels), jnp.bfloat16)] * count,
        (cells // step_cells,),
    )


def spectral_step(chunks, place, fwd, inv, w1, b1, w2, b2, together=2):
    count = len(chunks)
    sources, slots, _, width = chunks[0].shape
    channels = width // 2
    sizes = [sources * g.shape[2] for g in chunks]
    total = sum(sizes)
    keep = total // 2

    def kernel(place_ref, *refs):
        gs, (fwd_ref, inv_ref, w1_ref, b1_ref, w2_ref, b2_ref) = refs[:count], refs[count : count + 6]
        outs = refs[count + 6 :]

        def waves(u):
            sums = jnp.concatenate([g[:, u].reshape(size, width) for g, size in zip(gs, sizes)], axis=0)
            return dot32(fwd_ref[...], sums)

        def mix(u, both):
            cc, sc = both[:keep, :channels], both[:keep, channels:]
            cs, ss = both[keep:, :channels], both[keep:, channels:]
            single = (place_ref[1] + pl.program_id(0) * together + u) == 0
            upper = [jnp.where(single, cc, cc + ss), jnp.where(single, cs, cs - sc)]
            lower = [jnp.where(single, sc, cc - ss), jnp.where(single, ss, cs + sc)]
            modes = [jnp.concatenate([v.astype(jnp.bfloat16) for v in part], axis=1) for part in (upper, lower)]
            modes = jnp.concatenate(modes, axis=0)
            hidden = jnp.maximum((dot32(modes, w1_ref[...]) + b1_ref[...]).astype(jnp.bfloat16), 0)
            value = dot32(hidden, w2_ref[...]) + b2_ref[...]
            mixed = value - jnp.clip(value, -shrink_level, shrink_level)
            a, b = mixed[:keep, :channels], mixed[:keep, channels:]
            c, d = mixed[keep:, :channels], mixed[keep:, channels:]
            cos_part = [jnp.where(single, a, a + c), jnp.where(single, c, d - b)]
            sin_part = [jnp.where(single, b, b + d), jnp.where(single, d, a - c)]
            coefs = [jnp.concatenate([v.astype(jnp.bfloat16) for v in part], axis=1) for part in (cos_part, sin_part)]
            return jnp.concatenate(coefs, axis=0)

        def back(u, coefs):
            lines = dot32(inv_ref[...], coefs).astype(jnp.bfloat16)
            first = 0
            for out_ref, size in zip(outs, sizes):
                out_ref[:, u] = lines[first : first + size].reshape(sources, size // sources, width)
                first += size

        both = [waves(u) for u in range(together)]
        coefs = [mix(u, both[u]) for u in range(together)]
        for u in range(together):
            back(u, coefs[u])

    def block(g):
        return pl.BlockSpec((sources, together) + g.shape[2:], lambda i, p: (0, i, 0, 0))

    tables = [fwd, inv, w1, b1, w2, b2]
    return call(
        kernel,
        place,
        [*chunks, *tables],
        [block(g) for g in chunks] + [pl.BlockSpec(v.shape, lambda i, p: (0, 0)) for v in tables],
        [block(g) for g in chunks],
        [jax.ShapeDtypeStruct(g.shape, jnp.bfloat16) for g in chunks],
        (slots // together,),
        mib=48,
    )


def complex_weights(weights):
    real, imag = weights[0, 0], weights[1, 0]
    return jnp.concatenate(
        [jnp.concatenate([real, imag], axis=1), jnp.concatenate([-imag, real], axis=1)], axis=0
    )


def swap(part, axis, bits):
    return lax.ppermute(part, axis, [(j, j ^ bits) for j in range(lax.axis_size(axis))])


def swap_chips(parts):
    return [parts[0]] + [swap(parts[d], "lat", 2 * d) for d in range(1, len(parts))]


def swap_all(parts):
    return lax.all_to_all(parts, ("lat", "lon"), split_axis=0, concat_axis=0, tiled=True)


def swap_lat(parts):
    return lax.all_to_all(parts, "lat", split_axis=0, concat_axis=0, tiled=True)


def chunk_sizes(cells):
    return [cells // 2, cells // 2]


def lat_first_body(features, w_first, bias_first, w_second, bias_second):
    rows, lon_cells, channels = features.shape
    lat_count, lon_count = lax.axis_size("lat"), lax.axis_size("lon")
    total_lat, total_lon = rows * lat_count, lon_cells * lon_count
    devices, chips = lat_count * lon_count, lat_count // 2
    block_cells = lon_cells // lat_count
    slots = total_lat // 2 // devices
    norm = 1.0 / math.sqrt(total_lat * total_lon)
    sizes = chunk_sizes(block_cells)
    count = len(sizes)
    starts = [sum(sizes[:i]) for i in range(count)]
    cell_index = np.arange(total_lon).reshape(lon_count, lat_count, block_cells).transpose(1, 0, 2)
    order = [cell_index[..., s : s + n].reshape(-1) for s, n in zip(starts, sizes)]
    lat_fwd, lat_inv = lat_tables(total_lat, lat_count, norm)
    lon_fwd, lon_inv = lon_tables(np.concatenate(order), total_lon, norm)
    lat_place = lax.axis_index("lat")
    first_slot = (lat_place * lon_count + lax.axis_index("lon")) * slots
    place = jnp.stack([lat_place, first_slot]).astype(jnp.int32)
    own_fwd = lax.dynamic_index_in_dim(lat_fwd, lat_place, 0, keepdims=False)
    own_inv = lax.dynamic_index_in_dim(lat_inv, lat_place, 0, keepdims=False)
    w1, w2 = complex_weights(w_first), complex_weights(w_second)
    b1, b2 = bias_first.reshape(1, -1), bias_second.reshape(1, -1)
    tie = lax.optimization_barrier
    field = features.reshape(rows, chips, 2, block_cells, channels)

    def slot_sums(parts, table, i):
        part = lat_forward(parts, table, place)
        return swap_all(part.reshape(devices, slots, sizes[i], 2 * channels))

    first = split_all(field, place, starts[0], sizes[0])
    later, first = tie((field, first))
    for_twin = lax.dynamic_slice(
        later, (0, 0, 1 - lat_place % 2, starts[1], 0), (rows, chips, 1, sizes[1], channels)
    )
    twin = swap(for_twin.reshape(rows, chips, sizes[1], channels), "lat", 1)
    second = split_rows(later, twin, place, starts[1], sizes[1])
    first, second = tie((swap_lat(first), second))
    sums = [slot_sums([first], lat_fwd[0], 0), slot_sums(swap_chips(second), own_fwd, 1)]

    coefs = spectral_step(sums, place, lon_fwd, lon_inv, w1, b1, w2, b2)

    second = swap_all(coefs[1]).reshape(devices * slots, sizes[1], 2 * channels)
    second = swap_chips(lat_back(second, own_inv, place, 2, chips))
    first = swap_all(coefs[0]).reshape(devices * slots, sizes[0], 2 * channels)
    first, second = tie((first, second))
    first = lat_back(first, lat_inv[0], place, lat_count, 1)[0]
    first, second = tie((first, second))
    first = swap_lat(first)
    result, for_twin = join_own(field, second, place, starts[1], None)
    result = join_twin(field, swap(for_twin, "lat", 1), place, starts[1], result)
    result = join_all(field, first, place, starts[0], result)
    return result.reshape(features.shape)


def body(features, w_first, bias_first, w_second, bias_second):
    rows, lon_cells, channels = features.shape
    lat_count, lon_count = lax.axis_size("lat"), lax.axis_size("lon")
    fits = (
        (rows * lat_count // 2) % (lat_count * lon_count) == 0
        and lat_count & (lat_count - 1) == 0
        and lat_count > 1
        and lon_cells % (32 * lat_count) == 0
        and rows % 64 == 0
        and channels == 128
        and w_first.shape[1] == 1
    )
    chosen = lat_first_body if fits else general_body
    return chosen(features, w_first, bias_first, w_second, bias_second)


def solution(mesh):
    in_specs = (P("lat", "lon", None), P(), P(), P(), P())
    out_specs = P("lat", "lon", None)
    return jax.shard_map(body, mesh=mesh, in_specs=in_specs, out_specs=out_specs, check_vma=False)
```

```python
import math

import jax
import jax.numpy as jnp
import numpy as np
from jax import lax
from jax.experimental import pallas as pl
from jax.experimental.pallas import tpu as pltpu
from jax.sharding import PartitionSpec as P

shrink_level = 0.01


def phase_pair(product, length, sign):
    angle_value = (product % length).astype(jnp.float32) * (sign * 2.0 * math.pi / length)
    return (jnp.cos(angle_value), jnp.sin(angle_value))


def index_outer(left_index, right_index):
    return left_index[:, None] * right_index[None, :]


def twin_dot(pattern, operand, phase_table):
    upper_part = phase_table.astype(jnp.bfloat16)
    lower_part = (phase_table - upper_part.astype(jnp.float32)).astype(jnp.bfloat16)
    return jnp.einsum(
        pattern, operand, upper_part, preferred_element_type=jnp.float32
    ) + jnp.einsum(pattern, operand, lower_part, preferred_element_type=jnp.float32)


def complex_table(pattern, real_part, imag_part, cos_table, sin_table):
    real_out = twin_dot(pattern, real_part, cos_table) - twin_dot(pattern, imag_part, sin_table)
    imag_out = twin_dot(pattern, real_part, sin_table) + twin_dot(pattern, imag_part, cos_table)
    return (real_out, imag_out)


def bit_reverse(number, levels):
    result = jnp.zeros_like(number)
    for bit_level in range(levels):
        result = result + number // 2**bit_level % 2 * 2 ** (levels - 1 - bit_level)
    return result


def local_sections(received, levels):
    full_shape = received.shape
    real_part = received.astype(jnp.float32)
    imag_part = jnp.zeros_like(real_part)
    real_half = received
    imag_half = imag_part.astype(jnp.bfloat16)
    for section_level in range(levels - 1, -1, -1):
        half_span = 2**section_level
        split_shape = (full_shape[0], full_shape[1] // (2 * half_span), 2, half_span) + full_shape[
            2:
        ]
        real_split = real_part.reshape(split_shape)
        imag_split = imag_part.reshape(split_shape)
        tw_cos, tw_sin = phase_pair(jnp.arange(half_span, dtype=jnp.int32), 2 * half_span, -1.0)
        tw_cos = tw_cos[None, None, :, None, None]
        tw_sin = tw_sin[None, None, :, None, None]
        sum_re = real_split[:, :, 0] + real_split[:, :, 1]
        sum_im = imag_split[:, :, 0] + imag_split[:, :, 1]
        diff_re = real_split[:, :, 0] - real_split[:, :, 1]
        diff_im = imag_split[:, :, 0] - imag_split[:, :, 1]
        upper_re = diff_re * tw_cos - diff_im * tw_sin
        upper_im = diff_re * tw_sin + diff_im * tw_cos
        real_half = jnp.stack([sum_re, upper_re], axis=2).reshape(full_shape).astype(jnp.bfloat16)
        imag_half = jnp.stack([sum_im, upper_im], axis=2).reshape(full_shape).astype(jnp.bfloat16)
        real_part = real_half.astype(jnp.float32)
        imag_part = imag_half.astype(jnp.float32)
    return (real_half, imag_half)


def block_product(real_part, imag_part, weights):
    real_out = jnp.einsum(
        "tnj,njk->tnk", real_part, weights[0], preferred_element_type=jnp.float32
    ) - jnp.einsum("tnj,njk->tnk", imag_part, weights[1], preferred_element_type=jnp.float32)
    imag_out = jnp.einsum(
        "tnj,njk->tnk", imag_part, weights[0], preferred_element_type=jnp.float32
    ) + jnp.einsum("tnj,njk->tnk", real_part, weights[1], preferred_element_type=jnp.float32)
    return (real_out, imag_out)


def soft_shrink(values):
    return jnp.sign(values) * jnp.maximum(jnp.abs(values) - shrink_level, 0.0)


def spectral_mix(real_part, imag_part, w_first, bias_first, w_second, bias_second):
    shape_in = real_part.shape
    blocks = w_first.shape[1]
    block_width = w_first.shape[2]
    flat_re = real_part.reshape(-1, blocks, block_width)
    flat_im = imag_part.reshape(-1, blocks, block_width)
    hid_re, hid_im = block_product(flat_re, flat_im, w_first)
    act_re = jax.nn.relu(hid_re + bias_first[0]).astype(jnp.bfloat16)
    act_im = jax.nn.relu(hid_im + bias_first[1]).astype(jnp.bfloat16)
    out_re, out_im = block_product(act_re, act_im, w_second)
    return (
        soft_shrink(out_re + bias_second[0]).astype(jnp.bfloat16).reshape(shape_in),
        soft_shrink(out_im + bias_second[1]).astype(jnp.bfloat16).reshape(shape_in),
    )


def send_real(blocks):
    return lax.all_to_all(blocks, "lon", split_axis=1, concat_axis=1, tiled=True)


def to_columns(real_part, imag_part):
    return (
        lax.all_to_all(real_part, "lat", split_axis=1, concat_axis=0, tiled=True),
        lax.all_to_all(imag_part, "lat", split_axis=1, concat_axis=0, tiled=True),
    )


def to_rows(real_part, imag_part):
    return (
        lax.all_to_all(real_part, "lat", split_axis=0, concat_axis=1, tiled=True),
        lax.all_to_all(imag_part, "lat", split_axis=0, concat_axis=1, tiled=True),
    )


def general_body(features, w_first, bias_first, w_second, bias_second):
    lat_rows, lon_cells, channels = features.shape
    lon_count = lax.axis_size("lon")
    lat_count = lax.axis_size("lat")
    total_lat = lat_rows * lat_count
    total_lon = lon_cells * lon_count
    stride = lon_cells // lon_count
    keep_cells = lon_cells // 2
    norm_factor = 1.0 / math.sqrt(total_lat * total_lon)
    levels = lon_count.bit_length() - 1
    lon_place = lax.axis_index("lon")
    shard_index = jnp.arange(lon_count, dtype=jnp.int32)
    cell_index = jnp.arange(lon_cells, dtype=jnp.int32)
    keep_index = jnp.arange(keep_cells, dtype=jnp.int32)
    own_freq = bit_reverse(lon_place, levels)
    source_freq = bit_reverse(shard_index, levels)
    received = send_real(features.reshape(lat_rows, lon_count, stride, channels))
    sectioned_re, sectioned_im = local_sections(received, levels)
    cell_local = lon_place * stride + jnp.arange(stride, dtype=jnp.int32)
    rot_cos, rot_sin = phase_pair(index_outer(source_freq, cell_local), total_lon, -1.0)
    rot_cos = rot_cos[None, :, :, None]
    rot_sin = rot_sin[None, :, :, None]
    section_re = sectioned_re.astype(jnp.float32)
    section_im = sectioned_im.astype(jnp.float32)
    first_re = (section_re * rot_cos - section_im * rot_sin).astype(jnp.bfloat16)
    first_im = (section_re * rot_sin + section_im * rot_cos).astype(jnp.bfloat16)
    first_re, first_im = (
        lax.all_to_all(first_re, "lon", split_axis=1, concat_axis=1, tiled=True),
        lax.all_to_all(first_im, "lon", split_axis=1, concat_axis=1, tiled=True),
    )
    first_re = first_re.reshape(lat_rows, lon_cells, channels)
    first_im = first_im.reshape(lat_rows, lon_cells, channels)
    wave_cos, wave_sin = phase_pair(index_outer(cell_index, keep_index), lon_cells, -1.0)
    lon_re, lon_im = complex_table("rmc,mq->rqc", first_re, first_im, wave_cos, wave_sin)
    col_re, col_im = to_columns(lon_re.astype(jnp.bfloat16), lon_im.astype(jnp.bfloat16))
    row_index = jnp.arange(total_lat, dtype=jnp.int32)
    lat_cos, lat_sin = phase_pair(index_outer(row_index, row_index), total_lat, -1.0)
    spec_re, spec_im = complex_table("rqc,rl->lqc", col_re, col_im, lat_cos, lat_sin)
    spec_re = (spec_re * norm_factor).astype(jnp.bfloat16)
    spec_im = (spec_im * norm_factor).astype(jnp.bfloat16)
    mix_re, mix_im = spectral_mix(spec_re, spec_im, w_first, bias_first, w_second, bias_second)
    back_re, back_im = complex_table("lqc,lr->rqc", mix_re, mix_im, lat_cos, -lat_sin)
    back_re, back_im = to_rows(back_re.astype(jnp.bfloat16), back_im.astype(jnp.bfloat16))
    mode_weight = jnp.where((own_freq == 0) & (keep_index == 0), 1.0, 2.0).astype(jnp.float32)
    inv_cos, inv_sin = phase_pair(index_outer(keep_index, cell_index), lon_cells, 1.0)
    inv_cos = inv_cos * mode_weight[:, None]
    inv_sin = inv_sin * mode_weight[:, None]
    inv_re, inv_im = complex_table("rqc,qm->rmc", back_re, back_im, inv_cos, inv_sin)
    turn_cos, turn_sin = phase_pair(cell_index * own_freq, total_lon, 1.0)
    turn_cos = turn_cos[None, :, None]
    turn_sin = turn_sin[None, :, None]
    lon_back_re = (inv_re * turn_cos - inv_im * turn_sin).astype(jnp.bfloat16)
    lon_back_im = (inv_re * turn_sin + inv_im * turn_cos).astype(jnp.bfloat16)
    lon_back_re = lon_back_re.reshape(lat_rows, lon_count, stride, channels)
    lon_back_im = lon_back_im.reshape(lat_rows, lon_count, stride, channels)
    got_re, got_im = (
        lax.all_to_all(lon_back_re, "lon", split_axis=1, concat_axis=1, tiled=True),
        lax.all_to_all(lon_back_im, "lon", split_axis=1, concat_axis=1, tiled=True),
    )
    back_cos, back_sin = phase_pair(index_outer(source_freq, shard_index), lon_count, 1.0)
    spatial = twin_dot("rxsc,xb->rbsc", got_re, back_cos) - twin_dot(
        "rxsc,xb->rbsc", got_im, back_sin
    )
    filtered = (spatial * norm_factor).astype(jnp.bfloat16)
    filtered = send_real(filtered).reshape(lat_rows, lon_cells, channels)
    return (features.astype(jnp.float32) + filtered.astype(jnp.float32)).astype(jnp.bfloat16)


def lat_tables(total_lat, scale, order):
    row = np.arange(total_lat)
    angle = (np.outer(np.arange(total_lat // 2), row) % total_lat) * (2.0 * np.pi / total_lat)
    sin_part = np.sin(angle)
    sin_part[0] = np.where(row % 2 == 0, 1.0, -1.0)
    forward = np.concatenate([np.cos(angle)[order], sin_part[order]], axis=0)
    return forward.astype(jnp.bfloat16), (forward.T * scale).astype(jnp.bfloat16)


def lon_tables(cell_order, total_lon, scale):
    keep = total_lon // 2
    angle = (np.outer(np.arange(keep), cell_order) % total_lon) * (2.0 * np.pi / total_lon)
    forward = np.concatenate([np.cos(angle), -np.sin(angle)], axis=0)
    weight = np.where(np.arange(keep) == 0, 1.0, 2.0)
    weight = np.concatenate([weight, weight])
    backward = (forward * weight[:, None]).T
    return jnp.asarray(forward * scale, jnp.bfloat16), jnp.asarray(backward, jnp.bfloat16)


def dot32(left, right):
    return jnp.dot(left, right, preferred_element_type=jnp.float32)


def turn(values):
    return jnp.transpose(values, (1, 0, 2))


def call(kernel, place, args, in_specs, out_specs, out_shape, grid, scratch=(), mib=24, alias=None):
    return pl.pallas_call(
        kernel,
        grid_spec=pltpu.PrefetchScalarGridSpec(
            num_scalar_prefetch=1,
            grid=grid,
            in_specs=in_specs,
            out_specs=out_specs,
            scratch_shapes=scratch,
        ),
        out_shape=out_shape,
        input_output_aliases=alias or {},
        compiler_params=pltpu.CompilerParams(vmem_limit_bytes=mib * 2**20),
        cost_estimate=pl.CostEstimate(flops=1, bytes_accessed=2**20, transcendentals=0),
    )(place, *args)


def split_all(features, place, start, cells, steps=4):
    rows, chips, cores, _, channels = features.shape
    tile = rows // steps

    def kernel(place_ref, x_ref, out_ref):
        for j in range(chips * cores):
            out_ref[j] = turn(x_ref[:, j // cores, j % cores])

    return call(
        kernel,
        place,
        [features],
        [pl.BlockSpec((tile, chips, cores, cells, channels), lambda i, p: (i, 0, 0, start // cells, 0))],
        pl.BlockSpec((chips * cores, cells, tile, channels), lambda i, p: (0, 0, i, 0)),
        jax.ShapeDtypeStruct((chips * cores, cells, rows, channels), jnp.bfloat16),
        (steps,),
    )


def join_all(features, part, place, start, partial, steps=4):
    rows, chips, cores, _, channels = features.shape
    cells = part.shape[1]
    tile = rows // steps

    def kernel(place_ref, x_ref, part_ref, *refs):
        out_ref = refs[-1]
        for j in range(chips * cores):
            at = (slice(None), j // cores, j % cores)
            added = x_ref[at].astype(jnp.float32) + turn(part_ref[j]).astype(jnp.float32)
            out_ref[at] = added.astype(jnp.bfloat16)

    block = pl.BlockSpec(
        (tile, chips, cores, cells, channels), lambda i, p: (i, 0, 0, start // cells, 0)
    )
    args = [features, part]
    specs = [block, pl.BlockSpec((chips * cores, cells, tile, channels), lambda i, p: (0, 0, i, 0))]
    alias = None
    if partial is not None:
        args, specs, alias = args + [partial], specs + [pl.BlockSpec(memory_space=pl.ANY)], {3: 0}
    shape = jax.ShapeDtypeStruct(features.shape, jnp.bfloat16)
    return call(kernel, place, args, specs, block, shape, (steps,), alias=alias)


def own_block(tile, chips, cells, start, flip):
    return pl.BlockSpec(
        (tile, chips, 1, cells, 128), lambda i, p: (i, 0, (p[0] % 2) ^ flip, start // cells, 0)
    )


def join_own(features, parts, place, start, partial, steps=4):
    rows, chips, _, _, channels = features.shape
    cells = parts[0].shape[1]
    tile = rows // steps

    def kernel(place_ref, x_ref, *refs):
        out_ref, twin_ref = refs[-2:]
        chip = place_ref[0] // 2
        for d in range(chips):
            added = x_ref[:, chip ^ d, 0].astype(jnp.float32) + turn(refs[d][0]).astype(jnp.float32)
            out_ref[:, chip ^ d, 0] = added.astype(jnp.bfloat16)
            twin_ref[:, chip ^ d] = turn(refs[d][1])

    block = own_block(tile, chips, cells, start, 0)
    part = pl.BlockSpec((2, cells, tile, channels), lambda i, p: (0, 0, i, 0))
    args, specs, alias = [features, *parts], [block] + [part] * chips, None
    if partial is not None:
        args, specs, alias = args + [partial], specs + [pl.BlockSpec(memory_space=pl.ANY)], {len(args) + 1: 0}
    return call(
        kernel,
        place,
        args,
        specs,
        [block, pl.BlockSpec((tile, chips, cells, channels), lambda i, p: (i, 0, 0, 0))],
        [
            jax.ShapeDtypeStruct(features.shape, jnp.bfloat16),
            jax.ShapeDtypeStruct((rows, chips, cells, channels), jnp.bfloat16),
        ],
        (steps,),
        alias=alias,
    )


def join_twin(features, twin, place, start, partial, steps=2):
    rows, chips, cells, channels = twin.shape
    tile = rows // steps

    def kernel(place_ref, x_ref, twin_ref, partial_ref, out_ref):
        added = x_ref[:, :, 0].astype(jnp.float32) + twin_ref[...].astype(jnp.float32)
        out_ref[:, :, 0] = added.astype(jnp.bfloat16)

    block = own_block(tile, chips, cells, start, 1)
    return call(
        kernel,
        place,
        [features, twin, partial],
        [
            block,
            pl.BlockSpec((tile, chips, cells, channels), lambda i, p: (i, 0, 0, 0)),
            pl.BlockSpec(memory_space=pl.ANY),
        ],
        block,
        jax.ShapeDtypeStruct(features.shape, jnp.bfloat16),
        (steps,),
        alias={3: 0},
    )


def lat_forward(part, table, place, step_cells=8):
    sources, cells, rows, channels = part.shape
    total = sources * rows
    half = total // 2

    def kernel(place_ref, x_ref, table_ref, out_ref):
        sums = lat_sums(x_ref, table_ref, step_cells)
        for t in range(2):
            lines = jnp.stack([v[t * half : (t + 1) * half] for v in sums], axis=0)
            out_ref[:, :, t * channels : (t + 1) * channels] = turn(lines)

    return call(
        kernel,
        place,
        [part, table],
        [
            pl.BlockSpec((sources, step_cells, rows, channels), lambda i, p: (0, i, 0, 0)),
            pl.BlockSpec((total, total), lambda i, p: (0, 0)),
        ],
        pl.BlockSpec((half, step_cells, 2 * channels), lambda i, p: (0, i, 0)),
        jax.ShapeDtypeStruct((half, cells, 2 * channels), jnp.bfloat16),
        (cells // step_cells,),
    )


def lat_sums(x_ref, table_ref, cells):
    sources, channels = x_ref.shape[0], x_ref.shape[3]
    sums = []
    for cell in range(0, cells, 2):
        pair = [jnp.concatenate([x_ref[j, cell + t] for j in range(sources)], axis=0) for t in range(2)]
        result = dot32(table_ref[...], jnp.concatenate(pair, axis=1)).astype(jnp.bfloat16)
        sums += [result[:, :channels], result[:, channels:]]
    return sums


def lat_forward_groups(part, table, place, groups):
    sources, cells, rows, channels = part.shape
    total = sources * rows
    half = total // 2
    size = half // groups

    def kernel(place_ref, x_ref, table_ref, *refs):
        outs, stage = refs[:-1], refs[-1]
        for cell, value in enumerate(lat_sums(x_ref, table_ref, cells)):
            stage[:, :, cell] = value.reshape(2, groups, size, channels)
        for e in range(groups):
            for t in range(2):
                outs[e][:, :, t * channels : (t + 1) * channels] = turn(stage[t, place_ref[2] ^ e])

    shape = (size, cells, 2 * channels)
    return call(
        kernel,
        place,
        [part, table],
        [pl.BlockSpec(part.shape, lambda i, p: (0, 0, 0, 0)), pl.BlockSpec((total, total), lambda i, p: (0, 0))],
        [pl.BlockSpec(shape, lambda i, p: (0, 0, 0))] * groups,
        [jax.ShapeDtypeStruct(shape, jnp.bfloat16)] * groups,
        (1,),
        [pltpu.VMEM((2, groups, cells, size, channels), jnp.bfloat16)],
    )


def lat_back(h, table, place, groups, count, step_cells=8):
    half, cells, width = h.shape
    channels = width // 2
    total = 2 * half
    rows = total // groups // count

    def kernel(place_ref, h_ref, table_ref, *outs):
        lines = [turn(h_ref[:, :, part * channels : (part + 1) * channels]) for part in range(2)]
        for cell in range(0, step_cells, 2):
            pair = [jnp.concatenate([v[cell + t] for v in lines], axis=0) for t in range(2)]
            result = dot32(table_ref[...], jnp.concatenate(pair, axis=1)).astype(jnp.bfloat16)
            for t in range(2):
                part = result[:, t * channels : (t + 1) * channels].reshape(count, groups, rows, channels)
                for d in range(count):
                    outs[d][:, cell + t] = part[d]

    return call(
        kernel,
        place,
        [h, table],
        [
            pl.BlockSpec((half, step_cells, width), lambda i, p: (0, i, 0)),
            pl.BlockSpec((total, total), lambda i, p: (0, 0)),
        ],
        [pl.BlockSpec((groups, step_cells, rows, channels), lambda i, p: (0, i, 0, 0))] * count,
        [jax.ShapeDtypeStruct((groups, cells, rows, channels), jnp.bfloat16)] * count,
        (cells // step_cells,),
    )


def merge(chunks, place):
    count, groups = len(chunks), len(chunks[0])
    targets, slots, cells, width = chunks[0][0].shape

    def kernel(place_ref, *refs):
        ins, outs = refs[: count * groups], refs[count * groups :]
        for d in range(targets):
            for c in range(count):
                for e in range(groups):
                    outs[d][e, :, c * cells : (c + 1) * cells] = ins[c * groups + e][place_ref[0] ^ d]

    shape = (groups, slots, count * cells, width)
    return call(
        kernel,
        place,
        [v for chunk in chunks for v in chunk],
        [pl.BlockSpec(chunks[0][0].shape, lambda i, p: (0, 0, 0, 0))] * (count * groups),
        [pl.BlockSpec(shape, lambda i, p: (0, 0, 0, 0))] * targets,
        [jax.ShapeDtypeStruct(shape, jnp.bfloat16)] * targets,
        (1,),
    )


def spectral_step(parts, chunk, place, fwd, inv, w1, b1, w2, b2, together=2):
    targets = len(parts)
    groups, slots, cells, width = parts[0].shape
    channels = width // 2
    sources, _, more, _ = chunk.shape
    first = targets * groups * cells
    total = first + sources * more
    keep = total // 2

    def kernel(place_ref, *refs):
        ins, g_ref, refs = refs[:targets], refs[targets], refs[targets + 1 :]
        fwd_ref, inv_ref, w1_ref, b1_ref, w2_ref, b2_ref = refs[:6]
        near_ref, out_ref, stage = refs[6:]
        pairs = [(d, e) for d in range(targets) for e in range(groups)]

        def waves(u):
            for d, e in pairs:
                stage[u, place_ref[0] ^ d, place_ref[2] ^ e] = ins[d][e, u]
            near = stage[u].reshape(first, width)
            sums = jnp.concatenate([near, g_ref[:, u].reshape(total - first, width)], axis=0)
            return dot32(fwd_ref[...], sums)

        def mix(u, both):
            cc, sc = both[:keep, :channels], both[:keep, channels:]
            cs, ss = both[keep:, :channels], both[keep:, channels:]
            single = (place_ref[1] + pl.program_id(0) * together + u) == 0
            upper = [jnp.where(single, cc, cc + ss), jnp.where(single, cs, cs - sc)]
            lower = [jnp.where(single, sc, cc - ss), jnp.where(single, ss, cs + sc)]
            modes = [jnp.concatenate([v.astype(jnp.bfloat16) for v in part], axis=1) for part in (upper, lower)]
            modes = jnp.concatenate(modes, axis=0)
            hidden = jnp.maximum((dot32(modes, w1_ref[...]) + b1_ref[...]).astype(jnp.bfloat16), 0)
            value = dot32(hidden, w2_ref[...]) + b2_ref[...]
            mixed = value - jnp.clip(value, -shrink_level, shrink_level)
            a, b = mixed[:keep, :channels], mixed[:keep, channels:]
            c, d = mixed[keep:, :channels], mixed[keep:, channels:]
            cos_part = [jnp.where(single, a, a + c), jnp.where(single, c, d - b)]
            sin_part = [jnp.where(single, b, b + d), jnp.where(single, d, a - c)]
            coefs = [jnp.concatenate([v.astype(jnp.bfloat16) for v in part], axis=1) for part in (cos_part, sin_part)]
            return jnp.concatenate(coefs, axis=0)

        def back(u, coefs):
            lines = dot32(inv_ref[...], coefs).astype(jnp.bfloat16)
            out_ref[:, u] = lines[first:].reshape(sources, more, width)
            near_ref[:, u] = lines[:first].reshape(sources, cells, width)

        both = [waves(u) for u in range(together)]
        coefs = [mix(u, both[u]) for u in range(together)]
        for u in range(together):
            back(u, coefs[u])

    near = pl.BlockSpec((groups, together, cells, width), lambda i, p: (0, i, 0, 0))
    block = pl.BlockSpec((sources, together, more, width), lambda i, p: (0, i, 0, 0))
    tables = [fwd, inv, w1, b1, w2, b2]
    return call(
        kernel,
        place,
        [*parts, chunk, *tables],
        [near] * targets + [block] + [pl.BlockSpec(v.shape, lambda i, p: (0, 0)) for v in tables],
        [pl.BlockSpec((sources, together, cells, width), lambda i, p: (0, i, 0, 0)), block],
        [jax.ShapeDtypeStruct((sources, slots, n, width), jnp.bfloat16) for n in (cells, more)],
        (slots // together,),
        [pltpu.VMEM((together, targets, groups, cells, width), jnp.bfloat16)],
        mib=48,
    )
def complex_weights(weights):
    real, imag = weights[0, 0], weights[1, 0]
    return jnp.concatenate(
        [jnp.concatenate([real, imag], axis=1), jnp.concatenate([-imag, real], axis=1)], axis=0
    )


def swap(parts, axis):
    return [parts[0]] + [swap_bits(parts[d], axis, d) for d in range(1, len(parts))]


def swap_bits(part, axis, bits):
    return lax.ppermute(part, axis, [(j, j ^ bits) for j in range(lax.axis_size(axis))])


def swap_chips(parts):
    return [parts[0]] + [swap_bits(parts[d], "lat", 2 * d) for d in range(1, len(parts))]


def swap_lat(parts):
    return lax.all_to_all(parts, "lat", split_axis=0, concat_axis=0, tiled=True)


def swap_all(parts):
    return lax.all_to_all(parts, ("lat", "lon"), split_axis=0, concat_axis=0, tiled=True)


def lat_first_body(features, w_first, bias_first, w_second, bias_second):
    rows, lon_cells, channels = features.shape
    lat_count, lon_count = lax.axis_size("lat"), lax.axis_size("lon")
    total_lat, total_lon = rows * lat_count, lon_cells * lon_count
    devices, width = lat_count * lon_count, 2 * channels
    block_cells = lon_cells // lat_count
    slots = total_lat // 2 // devices
    norm = 1.0 / math.sqrt(total_lat * total_lon)
    half = block_cells // 2
    sizes, starts = [half // 2, half // 2, half], [0, half // 2, half]
    cell_index = np.arange(total_lon).reshape(lon_count, lat_count, 2, half).transpose(2, 1, 0, 3)
    lon_fwd, lon_inv = lon_tables(cell_index.reshape(-1), total_lon, norm)
    slot_l = np.arange(total_lat // 2)
    lat_fwd, lat_inv = lat_tables(total_lat, norm, slot_l)
    by_lon = slot_l.reshape(lat_count, lon_count, slots).transpose(1, 0, 2).reshape(-1)
    lon_first_fwd, _ = lat_tables(total_lat, norm, by_lon)
    places = np.arange(lat_count)
    by_place = lat_inv.reshape(lat_count, rows, total_lat)
    own_inv = np.stack([by_place[p ^ places].reshape(lat_inv.shape) for p in range(lat_count)])
    lat_place, lon_place = lax.axis_index("lat"), lax.axis_index("lon")
    first_slot = (lat_place * lon_count + lon_place) * slots
    place = jnp.stack([lat_place, first_slot, lon_place]).astype(jnp.int32)
    own_inv = lax.dynamic_index_in_dim(jnp.asarray(own_inv), lat_place, 0, keepdims=False)
    w1, w2 = complex_weights(w_first), complex_weights(w_second)
    b1, b2 = bias_first.reshape(1, -1), bias_second.reshape(1, -1)
    tie = lax.optimization_barrier
    field = features.reshape(rows, lat_count // 2, 2, block_cells, channels)

    sent = split_all(field, place, starts[0], sizes[0])
    later, sent = tie((field, sent))
    waiting = [split_all(later, place, starts[i], sizes[i]) for i in (1, 2)]
    got, waiting = tie((swap_lat(sent), waiting))
    across = []
    for i in range(2):
        groups = lat_forward_groups(got, lon_first_fwd, place, lon_count)
        sent, groups = tie((waiting[i], groups))
        if across:
            sent, across[-1] = tie((sent, across[-1]))
        got = swap_lat(sent)
        across.append(swap(groups, "lon"))
    last = lat_forward(got, lat_fwd, place)
    last, across[-1] = tie((last, across[-1]))
    last = swap_all(last.reshape(devices, slots, sizes[2], width))
    near = [[v.reshape(lat_count, slots, sizes[0], width) for v in groups] for groups in across]
    near = swap(merge(near, place), "lat")

    near, last = spectral_step(near, last, place, lon_fwd, lon_inv, w1, b1, w2, b2)

    last = swap_all(last).reshape(devices * slots, half, width)
    last = swap_chips(lat_back(last, own_inv, place, 2, lat_count // 2))
    near = swap_all(near).reshape(devices * slots, half, width)
    near, last = tie((near, last))
    near = lat_back(near, lat_inv, place, lat_count, 1)[0]
    near, last = tie((near, last))
    near = swap_lat(near)
    result, for_twin = join_own(field, last, place, half, None)
    result = join_twin(field, swap_bits(for_twin, "lat", 1), place, half, result)
    result = join_all(field, near, place, 0, result)
    return result.reshape(features.shape)


def body(features, w_first, bias_first, w_second, bias_second):
    rows, lon_cells, channels = features.shape
    lat_count, lon_count = lax.axis_size("lat"), lax.axis_size("lon")
    fits = (
        (rows * lat_count) % (4 * lat_count * lon_count) == 0
        and lat_count & (lat_count - 1) == 0
        and lat_count > 1
        and lon_cells % (32 * lat_count) == 0
        and lon_count & (lon_count - 1) == 0
        and rows % 64 == 0
        and channels == 128
        and w_first.shape[1] == 1
    )
    chosen = lat_first_body if fits else general_body
    return chosen(features, w_first, bias_first, w_second, bias_second)


def solution(mesh):
    in_specs = (P("lat", "lon", None), P(), P(), P(), P())
    out_specs = P("lat", "lon", None)
    return jax.shard_map(body, mesh=mesh, in_specs=in_specs, out_specs=out_specs, check_vma=False)
```

```python
import math

import jax
import jax.numpy as jnp
import numpy as np
from jax import lax
from jax.experimental import pallas as pl
from jax.experimental.pallas import tpu as pltpu
from jax.sharding import PartitionSpec as P

shrink_level = 0.01


def phase_pair(product, length, sign):
    angle_value = (product % length).astype(jnp.float32) * (sign * 2.0 * math.pi / length)
    return (jnp.cos(angle_value), jnp.sin(angle_value))


def index_outer(left_index, right_index):
    return left_index[:, None] * right_index[None, :]


def twin_dot(pattern, operand, phase_table):
    upper_part = phase_table.astype(jnp.bfloat16)
    lower_part = (phase_table - upper_part.astype(jnp.float32)).astype(jnp.bfloat16)
    return jnp.einsum(
        pattern, operand, upper_part, preferred_element_type=jnp.float32
    ) + jnp.einsum(pattern, operand, lower_part, preferred_element_type=jnp.float32)


def complex_table(pattern, real_part, imag_part, cos_table, sin_table):
    real_out = twin_dot(pattern, real_part, cos_table) - twin_dot(pattern, imag_part, sin_table)
    imag_out = twin_dot(pattern, real_part, sin_table) + twin_dot(pattern, imag_part, cos_table)
    return (real_out, imag_out)


def bit_reverse(number, levels):
    result = jnp.zeros_like(number)
    for bit_level in range(levels):
        result = result + number // 2**bit_level % 2 * 2 ** (levels - 1 - bit_level)
    return result


def local_sections(received, levels):
    full_shape = received.shape
    real_part = received.astype(jnp.float32)
    imag_part = jnp.zeros_like(real_part)
    real_half = received
    imag_half = imag_part.astype(jnp.bfloat16)
    for section_level in range(levels - 1, -1, -1):
        half_span = 2**section_level
        split_shape = (full_shape[0], full_shape[1] // (2 * half_span), 2, half_span) + full_shape[
            2:
        ]
        real_split = real_part.reshape(split_shape)
        imag_split = imag_part.reshape(split_shape)
        tw_cos, tw_sin = phase_pair(jnp.arange(half_span, dtype=jnp.int32), 2 * half_span, -1.0)
        tw_cos = tw_cos[None, None, :, None, None]
        tw_sin = tw_sin[None, None, :, None, None]
        sum_re = real_split[:, :, 0] + real_split[:, :, 1]
        sum_im = imag_split[:, :, 0] + imag_split[:, :, 1]
        diff_re = real_split[:, :, 0] - real_split[:, :, 1]
        diff_im = imag_split[:, :, 0] - imag_split[:, :, 1]
        upper_re = diff_re * tw_cos - diff_im * tw_sin
        upper_im = diff_re * tw_sin + diff_im * tw_cos
        real_half = jnp.stack([sum_re, upper_re], axis=2).reshape(full_shape).astype(jnp.bfloat16)
        imag_half = jnp.stack([sum_im, upper_im], axis=2).reshape(full_shape).astype(jnp.bfloat16)
        real_part = real_half.astype(jnp.float32)
        imag_part = imag_half.astype(jnp.float32)
    return (real_half, imag_half)


def block_product(real_part, imag_part, weights):
    real_out = jnp.einsum(
        "tnj,njk->tnk", real_part, weights[0], preferred_element_type=jnp.float32
    ) - jnp.einsum("tnj,njk->tnk", imag_part, weights[1], preferred_element_type=jnp.float32)
    imag_out = jnp.einsum(
        "tnj,njk->tnk", imag_part, weights[0], preferred_element_type=jnp.float32
    ) + jnp.einsum("tnj,njk->tnk", real_part, weights[1], preferred_element_type=jnp.float32)
    return (real_out, imag_out)


def soft_shrink(values):
    return jnp.sign(values) * jnp.maximum(jnp.abs(values) - shrink_level, 0.0)


def spectral_mix(real_part, imag_part, w_first, bias_first, w_second, bias_second):
    shape_in = real_part.shape
    blocks = w_first.shape[1]
    block_width = w_first.shape[2]
    flat_re = real_part.reshape(-1, blocks, block_width)
    flat_im = imag_part.reshape(-1, blocks, block_width)
    hid_re, hid_im = block_product(flat_re, flat_im, w_first)
    act_re = jax.nn.relu(hid_re + bias_first[0]).astype(jnp.bfloat16)
    act_im = jax.nn.relu(hid_im + bias_first[1]).astype(jnp.bfloat16)
    out_re, out_im = block_product(act_re, act_im, w_second)
    return (
        soft_shrink(out_re + bias_second[0]).astype(jnp.bfloat16).reshape(shape_in),
        soft_shrink(out_im + bias_second[1]).astype(jnp.bfloat16).reshape(shape_in),
    )


def send_real(blocks):
    return lax.all_to_all(blocks, "lon", split_axis=1, concat_axis=1, tiled=True)


def to_columns(real_part, imag_part):
    return (
        lax.all_to_all(real_part, "lat", split_axis=1, concat_axis=0, tiled=True),
        lax.all_to_all(imag_part, "lat", split_axis=1, concat_axis=0, tiled=True),
    )


def to_rows(real_part, imag_part):
    return (
        lax.all_to_all(real_part, "lat", split_axis=0, concat_axis=1, tiled=True),
        lax.all_to_all(imag_part, "lat", split_axis=0, concat_axis=1, tiled=True),
    )


def general_body(features, w_first, bias_first, w_second, bias_second):
    lat_rows, lon_cells, channels = features.shape
    lon_count = lax.axis_size("lon")
    lat_count = lax.axis_size("lat")
    total_lat = lat_rows * lat_count
    total_lon = lon_cells * lon_count
    stride = lon_cells // lon_count
    keep_cells = lon_cells // 2
    norm_factor = 1.0 / math.sqrt(total_lat * total_lon)
    levels = lon_count.bit_length() - 1
    lon_place = lax.axis_index("lon")
    shard_index = jnp.arange(lon_count, dtype=jnp.int32)
    cell_index = jnp.arange(lon_cells, dtype=jnp.int32)
    keep_index = jnp.arange(keep_cells, dtype=jnp.int32)
    own_freq = bit_reverse(lon_place, levels)
    source_freq = bit_reverse(shard_index, levels)
    received = send_real(features.reshape(lat_rows, lon_count, stride, channels))
    sectioned_re, sectioned_im = local_sections(received, levels)
    cell_local = lon_place * stride + jnp.arange(stride, dtype=jnp.int32)
    rot_cos, rot_sin = phase_pair(index_outer(source_freq, cell_local), total_lon, -1.0)
    rot_cos = rot_cos[None, :, :, None]
    rot_sin = rot_sin[None, :, :, None]
    section_re = sectioned_re.astype(jnp.float32)
    section_im = sectioned_im.astype(jnp.float32)
    first_re = (section_re * rot_cos - section_im * rot_sin).astype(jnp.bfloat16)
    first_im = (section_re * rot_sin + section_im * rot_cos).astype(jnp.bfloat16)
    first_re, first_im = (
        lax.all_to_all(first_re, "lon", split_axis=1, concat_axis=1, tiled=True),
        lax.all_to_all(first_im, "lon", split_axis=1, concat_axis=1, tiled=True),
    )
    first_re = first_re.reshape(lat_rows, lon_cells, channels)
    first_im = first_im.reshape(lat_rows, lon_cells, channels)
    wave_cos, wave_sin = phase_pair(index_outer(cell_index, keep_index), lon_cells, -1.0)
    lon_re, lon_im = complex_table("rmc,mq->rqc", first_re, first_im, wave_cos, wave_sin)
    col_re, col_im = to_columns(lon_re.astype(jnp.bfloat16), lon_im.astype(jnp.bfloat16))
    row_index = jnp.arange(total_lat, dtype=jnp.int32)
    lat_cos, lat_sin = phase_pair(index_outer(row_index, row_index), total_lat, -1.0)
    spec_re, spec_im = complex_table("rqc,rl->lqc", col_re, col_im, lat_cos, lat_sin)
    spec_re = (spec_re * norm_factor).astype(jnp.bfloat16)
    spec_im = (spec_im * norm_factor).astype(jnp.bfloat16)
    mix_re, mix_im = spectral_mix(spec_re, spec_im, w_first, bias_first, w_second, bias_second)
    back_re, back_im = complex_table("lqc,lr->rqc", mix_re, mix_im, lat_cos, -lat_sin)
    back_re, back_im = to_rows(back_re.astype(jnp.bfloat16), back_im.astype(jnp.bfloat16))
    mode_weight = jnp.where((own_freq == 0) & (keep_index == 0), 1.0, 2.0).astype(jnp.float32)
    inv_cos, inv_sin = phase_pair(index_outer(keep_index, cell_index), lon_cells, 1.0)
    inv_cos = inv_cos * mode_weight[:, None]
    inv_sin = inv_sin * mode_weight[:, None]
    inv_re, inv_im = complex_table("rqc,qm->rmc", back_re, back_im, inv_cos, inv_sin)
    turn_cos, turn_sin = phase_pair(cell_index * own_freq, total_lon, 1.0)
    turn_cos = turn_cos[None, :, None]
    turn_sin = turn_sin[None, :, None]
    lon_back_re = (inv_re * turn_cos - inv_im * turn_sin).astype(jnp.bfloat16)
    lon_back_im = (inv_re * turn_sin + inv_im * turn_cos).astype(jnp.bfloat16)
    lon_back_re = lon_back_re.reshape(lat_rows, lon_count, stride, channels)
    lon_back_im = lon_back_im.reshape(lat_rows, lon_count, stride, channels)
    got_re, got_im = (
        lax.all_to_all(lon_back_re, "lon", split_axis=1, concat_axis=1, tiled=True),
        lax.all_to_all(lon_back_im, "lon", split_axis=1, concat_axis=1, tiled=True),
    )
    back_cos, back_sin = phase_pair(index_outer(source_freq, shard_index), lon_count, 1.0)
    spatial = twin_dot("rxsc,xb->rbsc", got_re, back_cos) - twin_dot(
        "rxsc,xb->rbsc", got_im, back_sin
    )
    filtered = (spatial * norm_factor).astype(jnp.bfloat16)
    filtered = send_real(filtered).reshape(lat_rows, lon_cells, channels)
    return (features.astype(jnp.float32) + filtered.astype(jnp.float32)).astype(jnp.bfloat16)


def lat_tables(total_lat, scale, order):
    row = np.arange(total_lat)
    angle = (np.outer(np.arange(total_lat // 2), row) % total_lat) * (2.0 * np.pi / total_lat)
    sin_part = np.sin(angle)
    sin_part[0] = np.where(row % 2 == 0, 1.0, -1.0)
    forward = np.concatenate([np.cos(angle)[order], sin_part[order]], axis=0)
    return forward.astype(jnp.bfloat16), (forward.T * scale).astype(jnp.bfloat16)


def lon_tables(cell_order, total_lon, scale):
    forward, backward = [], []
    for odd in range(2):
        waves = np.arange(odd, total_lon // 2, 2)
        angle = (np.outer(waves, cell_order) % total_lon) * (2.0 * np.pi / total_lon)
        table = np.concatenate([np.cos(angle), -np.sin(angle)], axis=0)
        weight = np.where(waves == 0, 1.0, 2.0)
        forward.append(table * scale)
        backward.append((table * np.concatenate([weight, weight])[:, None]).T)
    return jnp.asarray(np.stack(forward), jnp.bfloat16), jnp.asarray(np.stack(backward), jnp.bfloat16)


def dot32(left, right):
    return jnp.dot(left, right, preferred_element_type=jnp.float32)


def turn(values):
    return jnp.transpose(values, (1, 0, 2))


def call(kernel, place, args, in_specs, out_specs, out_shape, grid, scratch=(), mib=24, alias=None):
    return pl.pallas_call(
        kernel,
        grid_spec=pltpu.PrefetchScalarGridSpec(
            num_scalar_prefetch=1,
            grid=grid,
            in_specs=in_specs,
            out_specs=out_specs,
            scratch_shapes=scratch,
        ),
        out_shape=out_shape,
        input_output_aliases=alias or {},
        compiler_params=pltpu.CompilerParams(vmem_limit_bytes=mib * 2**20),
        cost_estimate=pl.CostEstimate(flops=1, bytes_accessed=2**20, transcendentals=0),
    )(place, *args)


def split_all(features, place, start, cells, steps=4):
    rows, chips, cores, _, channels = features.shape
    tile = rows // steps

    def kernel(place_ref, x_ref, out_ref):
        for j in range(chips * cores):
            out_ref[j] = turn(x_ref[:, j // cores, j % cores])

    return call(
        kernel,
        place,
        [features],
        [pl.BlockSpec((tile, chips, cores, cells, channels), lambda i, p: (i, 0, 0, start // cells, 0))],
        pl.BlockSpec((chips * cores, cells, tile, channels), lambda i, p: (0, 0, i, 0)),
        jax.ShapeDtypeStruct((chips * cores, cells, rows, channels), jnp.bfloat16),
        (steps,),
    )


def join_all(features, part, place, start, partial, steps=4):
    rows, chips, cores, _, channels = features.shape
    cells = part.shape[1]
    tile = rows // steps

    def kernel(place_ref, x_ref, part_ref, *refs):
        out_ref = refs[-1]
        for j in range(chips * cores):
            at = (slice(None), j // cores, j % cores)
            added = x_ref[at].astype(jnp.float32) + turn(part_ref[j]).astype(jnp.float32)
            out_ref[at] = added.astype(jnp.bfloat16)

    block = pl.BlockSpec(
        (tile, chips, cores, cells, channels), lambda i, p: (i, 0, 0, start // cells, 0)
    )
    args = [features, part]
    specs = [block, pl.BlockSpec((chips * cores, cells, tile, channels), lambda i, p: (0, 0, i, 0))]
    alias = None
    if partial is not None:
        args, specs, alias = args + [partial], specs + [pl.BlockSpec(memory_space=pl.ANY)], {3: 0}
    shape = jax.ShapeDtypeStruct(features.shape, jnp.bfloat16)
    return call(
        kernel,
        place,
        args,
        specs,
        block,
        shape,
        (steps,),
        alias=alias,
    )


def own_block(tile, chips, cells, start, flip):
    return pl.BlockSpec(
        (tile, chips, 1, cells, 128), lambda i, p: (i, 0, (p[0] % 2) ^ flip, start // cells, 0)
    )


def join_own(features, parts, place, start, partial, steps=4):
    rows, chips, _, _, channels = features.shape
    cells = parts[0].shape[1]
    tile = rows // steps

    def kernel(place_ref, x_ref, *refs):
        out_ref, twin_ref = refs[-2:]
        chip = place_ref[0] // 2
        for d in range(chips):
            added = x_ref[:, chip ^ d, 0].astype(jnp.float32) + turn(refs[d][0]).astype(jnp.float32)
            out_ref[:, chip ^ d, 0] = added.astype(jnp.bfloat16)
            twin_ref[:, chip ^ d] = turn(refs[d][1])

    block = own_block(tile, chips, cells, start, 0)
    part = pl.BlockSpec((2, cells, tile, channels), lambda i, p: (0, 0, i, 0))
    args, specs, alias = [features, *parts], [block] + [part] * chips, None
    if partial is not None:
        args, specs, alias = args + [partial], specs + [pl.BlockSpec(memory_space=pl.ANY)], {len(args) + 1: 0}
    return call(
        kernel,
        place,
        args,
        specs,
        [block, pl.BlockSpec((tile, chips, cells, channels), lambda i, p: (i, 0, 0, 0))],
        [
            jax.ShapeDtypeStruct(features.shape, jnp.bfloat16),
            jax.ShapeDtypeStruct((rows, chips, cells, channels), jnp.bfloat16),
        ],
        (steps,),
        alias=alias,
    )


def join_twin(features, twin, place, start, partial, steps=2):
    rows, chips, cells, channels = twin.shape
    tile = rows // steps

    def kernel(place_ref, x_ref, twin_ref, partial_ref, out_ref):
        added = x_ref[:, :, 0].astype(jnp.float32) + twin_ref[...].astype(jnp.float32)
        out_ref[:, :, 0] = added.astype(jnp.bfloat16)

    block = own_block(tile, chips, cells, start, 1)
    return call(
        kernel,
        place,
        [features, twin, partial],
        [
            block,
            pl.BlockSpec((tile, chips, cells, channels), lambda i, p: (i, 0, 0, 0)),
            pl.BlockSpec(memory_space=pl.ANY),
        ],
        block,
        jax.ShapeDtypeStruct(features.shape, jnp.bfloat16),
        (steps,),
        alias={3: 0},
    )


def lat_forward(part, table, place, step_cells=8):
    sources, cells, rows, channels = part.shape
    total = sources * rows
    half = total // 2

    def kernel(place_ref, x_ref, table_ref, out_ref):
        sums = lat_sums(x_ref, table_ref, step_cells)
        for t in range(2):
            lines = jnp.stack([v[t * half : (t + 1) * half] for v in sums], axis=0)
            out_ref[:, :, t * channels : (t + 1) * channels] = turn(lines)

    return call(
        kernel,
        place,
        [part, table],
        [
            pl.BlockSpec((sources, step_cells, rows, channels), lambda i, p: (0, i, 0, 0)),
            pl.BlockSpec((total, total), lambda i, p: (0, 0)),
        ],
        pl.BlockSpec((half, step_cells, 2 * channels), lambda i, p: (0, i, 0)),
        jax.ShapeDtypeStruct((half, cells, 2 * channels), jnp.bfloat16),
        (cells // step_cells,),
    )


def lat_sums(x_ref, table_ref, cells):
    sources, channels = x_ref.shape[0], x_ref.shape[3]
    sums = []
    for cell in range(0, cells, 2):
        pair = [jnp.concatenate([x_ref[j, cell + t] for j in range(sources)], axis=0) for t in range(2)]
        result = dot32(table_ref[...], jnp.concatenate(pair, axis=1)).astype(jnp.bfloat16)
        sums += [result[:, :channels], result[:, channels:]]
    return sums


def lat_forward_groups(part, table, place, groups):
    sources, cells, rows, channels = part.shape
    total = sources * rows
    half = total // 2
    size = half // groups

    def kernel(place_ref, x_ref, table_ref, *refs):
        outs, stage = refs[:-1], refs[-1]
        for cell, value in enumerate(lat_sums(x_ref, table_ref, cells)):
            stage[:, :, cell] = value.reshape(2, groups, size, channels)
        for e in range(groups):
            for t in range(2):
                outs[e][:, :, t * channels : (t + 1) * channels] = turn(stage[t, place_ref[2] ^ e])

    shape = (size, cells, 2 * channels)
    return call(
        kernel,
        place,
        [part, table],
        [pl.BlockSpec(part.shape, lambda i, p: (0, 0, 0, 0)), pl.BlockSpec((total, total), lambda i, p: (0, 0))],
        [pl.BlockSpec(shape, lambda i, p: (0, 0, 0))] * groups,
        [jax.ShapeDtypeStruct(shape, jnp.bfloat16)] * groups,
        (1,),
        [pltpu.VMEM((2, groups, cells, size, channels), jnp.bfloat16)],
    )


def lat_back(h, table, place, groups, count, step_cells=8):
    half, cells, width = h.shape
    channels = width // 2
    total = 2 * half
    rows = total // groups // count

    def kernel(place_ref, h_ref, table_ref, *outs):
        lines = [turn(h_ref[:, :, part * channels : (part + 1) * channels]) for part in range(2)]
        for cell in range(0, step_cells, 2):
            pair = [jnp.concatenate([v[cell + t] for v in lines], axis=0) for t in range(2)]
            result = dot32(table_ref[...], jnp.concatenate(pair, axis=1)).astype(jnp.bfloat16)
            for t in range(2):
                part = result[:, t * channels : (t + 1) * channels].reshape(count, groups, rows, channels)
                for d in range(count):
                    outs[d][:, cell + t] = part[d]

    return call(
        kernel,
        place,
        [h, table],
        [
            pl.BlockSpec((half, step_cells, width), lambda i, p: (0, i, 0)),
            pl.BlockSpec((total, total), lambda i, p: (0, 0)),
        ],
        [pl.BlockSpec((groups, step_cells, rows, channels), lambda i, p: (0, i, 0, 0))] * count,
        [jax.ShapeDtypeStruct((groups, cells, rows, channels), jnp.bfloat16)] * count,
        (cells // step_cells,),
    )


def merge(chunks, place):
    count, groups = len(chunks), len(chunks[0])
    targets, slots, cells, width = chunks[0][0].shape

    def kernel(place_ref, *refs):
        ins, outs = refs[: count * groups], refs[count * groups :]
        for d in range(targets):
            for c in range(count):
                for e in range(groups):
                    outs[d][e, :, c * cells : (c + 1) * cells] = ins[c * groups + e][place_ref[0] ^ d]

    shape = (groups, slots, count * cells, width)
    return call(
        kernel,
        place,
        [v for chunk in chunks for v in chunk],
        [pl.BlockSpec(chunks[0][0].shape, lambda i, p: (0, 0, 0, 0))] * (count * groups),
        [pl.BlockSpec(shape, lambda i, p: (0, 0, 0, 0))] * targets,
        [jax.ShapeDtypeStruct(shape, jnp.bfloat16)] * targets,
        (1,),
    )


def whole(array):
    return pl.BlockSpec(array.shape, lambda i, p: (0,) * array.ndim)


def spectral_step(parts, chunk, place, fwd, inv, w1, b1, w2, b2, together=2):
    targets = len(parts)
    groups, slots, cells, width = parts[0].shape
    channels = width // 2
    sources, _, more, _ = chunk.shape
    first = targets * groups * cells // 2
    keep = fwd.shape[1] // 2

    def kernel(place_ref, *refs):
        ins, g_ref, refs = refs[:targets], refs[targets], refs[targets + 1 :]
        fwd_ref, inv_ref, w1_ref, b1_ref, w2_ref, b2_ref = refs[:6]
        near_ref, out_ref, stage = refs[6:]
        pairs = [(d, e) for d in range(targets) for e in range(groups)]

        def waves(u):
            for d, e in pairs:
                stage[u, place_ref[0] ^ d, place_ref[2] ^ e] = ins[d][e, u]
            near = stage[u]
            far = g_ref[:, u].reshape(targets, groups, more, width)
            halves = [
                jnp.concatenate([v[:, z : z + groups // 2].reshape(-1, width) for v in (near, far)], axis=0)
                for z in (0, groups // 2)
            ]
            return [dot32(fwd_ref[0], halves[0] + halves[1]), dot32(fwd_ref[1], halves[0] - halves[1])]

        def mix(u, both):
            cc, sc = both[:keep, :channels], both[:keep, channels:]
            cs, ss = both[keep:, :channels], both[keep:, channels:]
            single = (place_ref[1] + pl.program_id(0) * together + u) == 0
            upper = [jnp.where(single, cc, cc + ss), jnp.where(single, cs, cs - sc)]
            lower = [jnp.where(single, sc, cc - ss), jnp.where(single, ss, cs + sc)]
            modes = [jnp.concatenate([v.astype(jnp.bfloat16) for v in part], axis=1) for part in (upper, lower)]
            modes = jnp.concatenate(modes, axis=0)
            hidden = jnp.maximum((dot32(modes, w1_ref[...]) + b1_ref[...]).astype(jnp.bfloat16), 0)
            value = dot32(hidden, w2_ref[...]) + b2_ref[...]
            mixed = value - jnp.clip(value, -shrink_level, shrink_level)
            a, b = mixed[:keep, :channels], mixed[:keep, channels:]
            c, d = mixed[keep:, :channels], mixed[keep:, channels:]
            cos_part = [jnp.where(single, a, a + c), jnp.where(single, c, d - b)]
            sin_part = [jnp.where(single, b, b + d), jnp.where(single, d, a - c)]
            coefs = [jnp.concatenate([v.astype(jnp.bfloat16) for v in part], axis=1) for part in (cos_part, sin_part)]
            return jnp.concatenate(coefs, axis=0)

        def back(u, coefs):
            even, odd = dot32(inv_ref[0], coefs[0]), dot32(inv_ref[1], coefs[1])
            halves = [(even + odd).astype(jnp.bfloat16), (even - odd).astype(jnp.bfloat16)]
            for ref, rows in ((near_ref, slice(0, first)), (out_ref, slice(first, None))):
                parts = [v[rows].reshape(targets, groups // 2, -1, width) for v in halves]
                ref[:, u] = jnp.concatenate(parts, axis=1).reshape(sources, -1, width)

        both = [waves(u) for u in range(together)]
        coefs = [[mix(u, v) for v in both[u]] for u in range(together)]
        for u in range(together):
            back(u, coefs[u])

    near = pl.BlockSpec((groups, together, cells, width), lambda i, p: (0, i, 0, 0))
    block = pl.BlockSpec((sources, together, more, width), lambda i, p: (0, i, 0, 0))
    tables = [fwd, inv, w1, b1, w2, b2]
    return call(
        kernel,
        place,
        [*parts, chunk, *tables],
        [near] * targets + [block] + [whole(v) for v in tables],
        [pl.BlockSpec((sources, together, cells, width), lambda i, p: (0, i, 0, 0)), block],
        [jax.ShapeDtypeStruct((sources, slots, n, width), jnp.bfloat16) for n in (cells, more)],
        (slots // together,),
        [pltpu.VMEM((together, targets, groups, cells, width), jnp.bfloat16)],
        mib=62,
    )
def complex_weights(weights):
    real, imag = weights[0, 0], weights[1, 0]
    return jnp.concatenate(
        [jnp.concatenate([real, imag], axis=1), jnp.concatenate([-imag, real], axis=1)], axis=0
    )


def swap(parts, axis):
    return [parts[0]] + [swap_bits(parts[d], axis, d) for d in range(1, len(parts))]


def swap_bits(part, axis, bits):
    return lax.ppermute(part, axis, [(j, j ^ bits) for j in range(lax.axis_size(axis))])


def swap_chips(parts):
    return [parts[0]] + [swap_bits(parts[d], "lat", 2 * d) for d in range(1, len(parts))]


def swap_lat(parts):
    return lax.all_to_all(parts, "lat", split_axis=0, concat_axis=0, tiled=True)


def swap_all(parts):
    return lax.all_to_all(parts, ("lat", "lon"), split_axis=0, concat_axis=0, tiled=True)


def lat_first_body(features, w_first, bias_first, w_second, bias_second):
    rows, lon_cells, channels = features.shape
    lat_count, lon_count = lax.axis_size("lat"), lax.axis_size("lon")
    total_lat, total_lon = rows * lat_count, lon_cells * lon_count
    devices, width = lat_count * lon_count, 2 * channels
    block_cells = lon_cells // lat_count
    slots = total_lat // 2 // devices
    norm = 1.0 / math.sqrt(total_lat * total_lon)
    half = block_cells // 2
    sizes, starts = [half // 2, half // 2, half], [0, half // 2, half]
    cell_index = np.arange(total_lon).reshape(lon_count, lat_count, 2, half).transpose(2, 1, 0, 3)
    cell_index = cell_index[:, :, : lon_count // 2]
    lon_fwd, lon_inv = lon_tables(cell_index.reshape(-1), total_lon, norm)
    slot_l = np.arange(total_lat // 2)
    lat_fwd, lat_inv = lat_tables(total_lat, norm, slot_l)
    by_lon = slot_l.reshape(lat_count, lon_count, slots).transpose(1, 0, 2).reshape(-1)
    lon_first_fwd, _ = lat_tables(total_lat, norm, by_lon)
    places = np.arange(lat_count)
    by_place = lat_inv.reshape(lat_count, rows, total_lat)
    own_inv = np.stack([by_place[p ^ places].reshape(lat_inv.shape) for p in range(lat_count)])
    lat_place, lon_place = lax.axis_index("lat"), lax.axis_index("lon")
    first_slot = (lat_place * lon_count + lon_place) * slots
    place = jnp.stack([lat_place, first_slot, lon_place]).astype(jnp.int32)
    own_inv = lax.dynamic_index_in_dim(jnp.asarray(own_inv), lat_place, 0, keepdims=False)
    w1, w2 = complex_weights(w_first), complex_weights(w_second)
    b1, b2 = bias_first.reshape(1, -1), bias_second.reshape(1, -1)
    tie = lax.optimization_barrier
    field = features.reshape(rows, lat_count // 2, 2, block_cells, channels)

    sent = split_all(field, place, starts[0], sizes[0])
    later, sent = tie((field, sent))
    waiting = [split_all(later, place, starts[i], sizes[i]) for i in (1, 2)]
    got, waiting = tie((swap_lat(sent), waiting))
    across = []
    for i in range(2):
        groups = lat_forward_groups(got, lon_first_fwd, place, lon_count)
        sent, groups = tie((waiting[i], groups))
        if across:
            sent, across[-1] = tie((sent, across[-1]))
        got = swap_lat(sent)
        across.append(swap(groups, "lon"))
    last = lat_forward(got, lat_fwd, place)
    last, across[-1] = tie((last, across[-1]))
    last = swap_all(last.reshape(devices, slots, sizes[2], width))
    near = [[v.reshape(lat_count, slots, sizes[0], width) for v in groups] for groups in across]
    near = swap(merge(near, place), "lat")

    near, last = spectral_step(near, last, place, lon_fwd, lon_inv, w1, b1, w2, b2)

    last = swap_all(last).reshape(devices * slots, half, width)
    last = swap_chips(lat_back(last, own_inv, place, 2, lat_count // 2))
    near = swap_all(near).reshape(devices * slots, half, width)
    near, last = tie((near, last))
    near = lat_back(near, lat_inv, place, lat_count, 1)[0]
    near, last = tie((near, last))
    near = swap_lat(near)
    result, for_twin = join_own(field, last, place, half, None)
    result = join_twin(field, swap_bits(for_twin, "lat", 1), place, half, result)
    result = join_all(field, near, place, 0, result)
    return result.reshape(features.shape)


def body(features, w_first, bias_first, w_second, bias_second):
    rows, lon_cells, channels = features.shape
    lat_count, lon_count = lax.axis_size("lat"), lax.axis_size("lon")
    fits = (
        (rows * lat_count) % (4 * lat_count * lon_count) == 0
        and lat_count & (lat_count - 1) == 0
        and lat_count > 1
        and lon_cells % (32 * lat_count) == 0
        and lon_count & (lon_count - 1) == 0
        and lon_count > 1
        and rows % 64 == 0
        and channels == 128
        and w_first.shape[1] == 1
    )
    chosen = lat_first_body if fits else general_body
    return chosen(features, w_first, bias_first, w_second, bias_second)


def solution(mesh):
    in_specs = (P("lat", "lon", None), P(), P(), P(), P())
    out_specs = P("lat", "lon", None)
    return jax.shard_map(body, mesh=mesh, in_specs=in_specs, out_specs=out_specs, check_vma=False)
```

```python
import math

import jax
import jax.numpy as jnp
import numpy as np
from jax import lax
from jax.experimental import pallas as pl
from jax.experimental.pallas import tpu as pltpu
from jax.sharding import PartitionSpec as P

shrink_level = 0.01


def phase_pair(product, length, sign):
    angle_value = (product % length).astype(jnp.float32) * (sign * 2.0 * math.pi / length)
    return (jnp.cos(angle_value), jnp.sin(angle_value))


def index_outer(left_index, right_index):
    return left_index[:, None] * right_index[None, :]


def twin_dot(pattern, operand, phase_table):
    upper_part = phase_table.astype(jnp.bfloat16)
    lower_part = (phase_table - upper_part.astype(jnp.float32)).astype(jnp.bfloat16)
    return jnp.einsum(
        pattern, operand, upper_part, preferred_element_type=jnp.float32
    ) + jnp.einsum(pattern, operand, lower_part, preferred_element_type=jnp.float32)


def complex_table(pattern, real_part, imag_part, cos_table, sin_table):
    real_out = twin_dot(pattern, real_part, cos_table) - twin_dot(pattern, imag_part, sin_table)
    imag_out = twin_dot(pattern, real_part, sin_table) + twin_dot(pattern, imag_part, cos_table)
    return (real_out, imag_out)


def bit_reverse(number, levels):
    result = jnp.zeros_like(number)
    for bit_level in range(levels):
        result = result + number // 2**bit_level % 2 * 2 ** (levels - 1 - bit_level)
    return result


def local_sections(received, levels):
    full_shape = received.shape
    real_part = received.astype(jnp.float32)
    imag_part = jnp.zeros_like(real_part)
    real_half = received
    imag_half = imag_part.astype(jnp.bfloat16)
    for section_level in range(levels - 1, -1, -1):
        half_span = 2**section_level
        split_shape = (full_shape[0], full_shape[1] // (2 * half_span), 2, half_span) + full_shape[
            2:
        ]
        real_split = real_part.reshape(split_shape)
        imag_split = imag_part.reshape(split_shape)
        tw_cos, tw_sin = phase_pair(jnp.arange(half_span, dtype=jnp.int32), 2 * half_span, -1.0)
        tw_cos = tw_cos[None, None, :, None, None]
        tw_sin = tw_sin[None, None, :, None, None]
        sum_re = real_split[:, :, 0] + real_split[:, :, 1]
        sum_im = imag_split[:, :, 0] + imag_split[:, :, 1]
        diff_re = real_split[:, :, 0] - real_split[:, :, 1]
        diff_im = imag_split[:, :, 0] - imag_split[:, :, 1]
        upper_re = diff_re * tw_cos - diff_im * tw_sin
        upper_im = diff_re * tw_sin + diff_im * tw_cos
        real_half = jnp.stack([sum_re, upper_re], axis=2).reshape(full_shape).astype(jnp.bfloat16)
        imag_half = jnp.stack([sum_im, upper_im], axis=2).reshape(full_shape).astype(jnp.bfloat16)
        real_part = real_half.astype(jnp.float32)
        imag_part = imag_half.astype(jnp.float32)
    return (real_half, imag_half)


def block_product(real_part, imag_part, weights):
    real_out = jnp.einsum(
        "tnj,njk->tnk", real_part, weights[0], preferred_element_type=jnp.float32
    ) - jnp.einsum("tnj,njk->tnk", imag_part, weights[1], preferred_element_type=jnp.float32)
    imag_out = jnp.einsum(
        "tnj,njk->tnk", imag_part, weights[0], preferred_element_type=jnp.float32
    ) + jnp.einsum("tnj,njk->tnk", real_part, weights[1], preferred_element_type=jnp.float32)
    return (real_out, imag_out)


def soft_shrink(values):
    return jnp.sign(values) * jnp.maximum(jnp.abs(values) - shrink_level, 0.0)


def spectral_mix(real_part, imag_part, w_first, bias_first, w_second, bias_second):
    shape_in = real_part.shape
    blocks = w_first.shape[1]
    block_width = w_first.shape[2]
    flat_re = real_part.reshape(-1, blocks, block_width)
    flat_im = imag_part.reshape(-1, blocks, block_width)
    hid_re, hid_im = block_product(flat_re, flat_im, w_first)
    act_re = jax.nn.relu(hid_re + bias_first[0]).astype(jnp.bfloat16)
    act_im = jax.nn.relu(hid_im + bias_first[1]).astype(jnp.bfloat16)
    out_re, out_im = block_product(act_re, act_im, w_second)
    return (
        soft_shrink(out_re + bias_second[0]).astype(jnp.bfloat16).reshape(shape_in),
        soft_shrink(out_im + bias_second[1]).astype(jnp.bfloat16).reshape(shape_in),
    )


def send_real(blocks):
    return lax.all_to_all(blocks, "lon", split_axis=1, concat_axis=1, tiled=True)


def to_columns(real_part, imag_part):
    return (
        lax.all_to_all(real_part, "lat", split_axis=1, concat_axis=0, tiled=True),
        lax.all_to_all(imag_part, "lat", split_axis=1, concat_axis=0, tiled=True),
    )


def to_rows(real_part, imag_part):
    return (
        lax.all_to_all(real_part, "lat", split_axis=0, concat_axis=1, tiled=True),
        lax.all_to_all(imag_part, "lat", split_axis=0, concat_axis=1, tiled=True),
    )


def general_body(features, w_first, bias_first, w_second, bias_second):
    lat_rows, lon_cells, channels = features.shape
    lon_count = lax.axis_size("lon")
    lat_count = lax.axis_size("lat")
    total_lat = lat_rows * lat_count
    total_lon = lon_cells * lon_count
    stride = lon_cells // lon_count
    keep_cells = lon_cells // 2
    norm_factor = 1.0 / math.sqrt(total_lat * total_lon)
    levels = lon_count.bit_length() - 1
    lon_place = lax.axis_index("lon")
    shard_index = jnp.arange(lon_count, dtype=jnp.int32)
    cell_index = jnp.arange(lon_cells, dtype=jnp.int32)
    keep_index = jnp.arange(keep_cells, dtype=jnp.int32)
    own_freq = bit_reverse(lon_place, levels)
    source_freq = bit_reverse(shard_index, levels)
    received = send_real(features.reshape(lat_rows, lon_count, stride, channels))
    sectioned_re, sectioned_im = local_sections(received, levels)
    cell_local = lon_place * stride + jnp.arange(stride, dtype=jnp.int32)
    rot_cos, rot_sin = phase_pair(index_outer(source_freq, cell_local), total_lon, -1.0)
    rot_cos = rot_cos[None, :, :, None]
    rot_sin = rot_sin[None, :, :, None]
    section_re = sectioned_re.astype(jnp.float32)
    section_im = sectioned_im.astype(jnp.float32)
    first_re = (section_re * rot_cos - section_im * rot_sin).astype(jnp.bfloat16)
    first_im = (section_re * rot_sin + section_im * rot_cos).astype(jnp.bfloat16)
    first_re, first_im = (
        lax.all_to_all(first_re, "lon", split_axis=1, concat_axis=1, tiled=True),
        lax.all_to_all(first_im, "lon", split_axis=1, concat_axis=1, tiled=True),
    )
    first_re = first_re.reshape(lat_rows, lon_cells, channels)
    first_im = first_im.reshape(lat_rows, lon_cells, channels)
    wave_cos, wave_sin = phase_pair(index_outer(cell_index, keep_index), lon_cells, -1.0)
    lon_re, lon_im = complex_table("rmc,mq->rqc", first_re, first_im, wave_cos, wave_sin)
    col_re, col_im = to_columns(lon_re.astype(jnp.bfloat16), lon_im.astype(jnp.bfloat16))
    row_index = jnp.arange(total_lat, dtype=jnp.int32)
    lat_cos, lat_sin = phase_pair(index_outer(row_index, row_index), total_lat, -1.0)
    spec_re, spec_im = complex_table("rqc,rl->lqc", col_re, col_im, lat_cos, lat_sin)
    spec_re = (spec_re * norm_factor).astype(jnp.bfloat16)
    spec_im = (spec_im * norm_factor).astype(jnp.bfloat16)
    mix_re, mix_im = spectral_mix(spec_re, spec_im, w_first, bias_first, w_second, bias_second)
    back_re, back_im = complex_table("lqc,lr->rqc", mix_re, mix_im, lat_cos, -lat_sin)
    back_re, back_im = to_rows(back_re.astype(jnp.bfloat16), back_im.astype(jnp.bfloat16))
    mode_weight = jnp.where((own_freq == 0) & (keep_index == 0), 1.0, 2.0).astype(jnp.float32)
    inv_cos, inv_sin = phase_pair(index_outer(keep_index, cell_index), lon_cells, 1.0)
    inv_cos = inv_cos * mode_weight[:, None]
    inv_sin = inv_sin * mode_weight[:, None]
    inv_re, inv_im = complex_table("rqc,qm->rmc", back_re, back_im, inv_cos, inv_sin)
    turn_cos, turn_sin = phase_pair(cell_index * own_freq, total_lon, 1.0)
    turn_cos = turn_cos[None, :, None]
    turn_sin = turn_sin[None, :, None]
    lon_back_re = (inv_re * turn_cos - inv_im * turn_sin).astype(jnp.bfloat16)
    lon_back_im = (inv_re * turn_sin + inv_im * turn_cos).astype(jnp.bfloat16)
    lon_back_re = lon_back_re.reshape(lat_rows, lon_count, stride, channels)
    lon_back_im = lon_back_im.reshape(lat_rows, lon_count, stride, channels)
    got_re, got_im = (
        lax.all_to_all(lon_back_re, "lon", split_axis=1, concat_axis=1, tiled=True),
        lax.all_to_all(lon_back_im, "lon", split_axis=1, concat_axis=1, tiled=True),
    )
    back_cos, back_sin = phase_pair(index_outer(source_freq, shard_index), lon_count, 1.0)
    spatial = twin_dot("rxsc,xb->rbsc", got_re, back_cos) - twin_dot(
        "rxsc,xb->rbsc", got_im, back_sin
    )
    filtered = (spatial * norm_factor).astype(jnp.bfloat16)
    filtered = send_real(filtered).reshape(lat_rows, lon_cells, channels)
    return (features.astype(jnp.float32) + filtered.astype(jnp.float32)).astype(jnp.bfloat16)


def lat_tables(total_lat, scale, order):
    row = np.arange(total_lat)
    angle = (np.outer(np.arange(total_lat // 2), row) % total_lat) * (2.0 * np.pi / total_lat)
    sin_part = np.sin(angle)
    sin_part[0] = np.where(row % 2 == 0, 1.0, -1.0)
    forward = np.concatenate([np.cos(angle)[order], sin_part[order]], axis=0)
    return forward.astype(jnp.bfloat16), (forward.T * scale).astype(jnp.bfloat16)


def lon_tables(cell_order, total_lon, scale):
    forward, backward = [], []
    for odd in range(2):
        waves = np.arange(odd, total_lon // 2, 2)
        angle = (np.outer(waves, cell_order) % total_lon) * (2.0 * np.pi / total_lon)
        table = np.concatenate([np.cos(angle), -np.sin(angle)], axis=0)
        weight = np.where(waves == 0, 1.0, 2.0)
        forward.append(table * scale)
        backward.append((table * np.concatenate([weight, weight])[:, None]).T)
    return jnp.asarray(np.stack(forward), jnp.bfloat16), jnp.asarray(np.stack(backward), jnp.bfloat16)


def dot32(left, right):
    return jnp.dot(left, right, preferred_element_type=jnp.float32)


def turn(values):
    return jnp.transpose(values, (1, 0, 2))


def call(kernel, place, args, in_specs, out_specs, out_shape, grid, scratch=(), mib=24, alias=None):
    return pl.pallas_call(
        kernel,
        grid_spec=pltpu.PrefetchScalarGridSpec(
            num_scalar_prefetch=1,
            grid=grid,
            in_specs=in_specs,
            out_specs=out_specs,
            scratch_shapes=scratch,
        ),
        out_shape=out_shape,
        input_output_aliases=alias or {},
        compiler_params=pltpu.CompilerParams(vmem_limit_bytes=mib * 2**20),
        cost_estimate=pl.CostEstimate(flops=1, bytes_accessed=2**20, transcendentals=0),
    )(place, *args)


def split_all(features, place, start, cells, steps=4):
    rows, chips, cores, _, channels = features.shape
    tile = rows // steps

    def kernel(place_ref, x_ref, out_ref):
        for j in range(chips * cores):
            out_ref[j] = turn(x_ref[:, j // cores, j % cores])

    return call(
        kernel,
        place,
        [features],
        [pl.BlockSpec((tile, chips, cores, cells, channels), lambda i, p: (i, 0, 0, start // cells, 0))],
        pl.BlockSpec((chips * cores, cells, tile, channels), lambda i, p: (0, 0, i, 0)),
        jax.ShapeDtypeStruct((chips * cores, cells, rows, channels), jnp.bfloat16),
        (steps,),
    )


def join_all(features, part, place, start, partial, steps=2):
    rows, chips, cores, _, channels = features.shape
    cells = part.shape[1]
    tile = rows // steps

    def kernel(place_ref, x_ref, part_ref, *refs):
        out_ref = refs[-1]
        for j in range(chips * cores):
            at = (slice(None), j // cores, j % cores)
            added = x_ref[at].astype(jnp.float32) + turn(part_ref[j]).astype(jnp.float32)
            out_ref[at] = added.astype(jnp.bfloat16)

    block = pl.BlockSpec(
        (tile, chips, cores, cells, channels), lambda i, p: (i, 0, 0, start // cells, 0)
    )
    args = [features, part]
    specs = [block, pl.BlockSpec((chips * cores, cells, tile, channels), lambda i, p: (0, 0, i, 0))]
    alias = None
    if partial is not None:
        args, specs, alias = args + [partial], specs + [pl.BlockSpec(memory_space=pl.ANY)], {3: 0}
    shape = jax.ShapeDtypeStruct(features.shape, jnp.bfloat16)
    return call(
        kernel,
        place,
        args,
        specs,
        block,
        shape,
        (steps,),
        alias=alias,
    )


def own_block(tile, chips, cells, start, flip):
    return pl.BlockSpec(
        (tile, chips, 1, cells, 128), lambda i, p: (i, 0, (p[0] % 2) ^ flip, start // cells, 0)
    )


def join_own(features, parts, place, start, partial, steps=4):
    rows, chips, _, _, channels = features.shape
    cells = parts[0].shape[1]
    tile = rows // steps

    def kernel(place_ref, x_ref, *refs):
        out_ref, twin_ref = refs[-2:]
        chip = place_ref[0] // 2
        for d in range(chips):
            added = x_ref[:, chip ^ d, 0].astype(jnp.float32) + turn(refs[d][0]).astype(jnp.float32)
            out_ref[:, chip ^ d, 0] = added.astype(jnp.bfloat16)
            twin_ref[:, chip ^ d] = turn(refs[d][1])

    block = own_block(tile, chips, cells, start, 0)
    part = pl.BlockSpec((2, cells, tile, channels), lambda i, p: (0, 0, i, 0))
    args, specs, alias = [features, *parts], [block] + [part] * chips, None
    if partial is not None:
        args, specs, alias = args + [partial], specs + [pl.BlockSpec(memory_space=pl.ANY)], {len(args) + 1: 0}
    return call(
        kernel,
        place,
        args,
        specs,
        [block, pl.BlockSpec((tile, chips, cells, channels), lambda i, p: (i, 0, 0, 0))],
        [
            jax.ShapeDtypeStruct(features.shape, jnp.bfloat16),
            jax.ShapeDtypeStruct((rows, chips, cells, channels), jnp.bfloat16),
        ],
        (steps,),
        alias=alias,
    )


def join_twin(features, twin, place, start, partial, steps=2):
    rows, chips, cells, channels = twin.shape
    tile = rows // steps

    def kernel(place_ref, x_ref, twin_ref, partial_ref, out_ref):
        added = x_ref[:, :, 0].astype(jnp.float32) + twin_ref[...].astype(jnp.float32)
        out_ref[:, :, 0] = added.astype(jnp.bfloat16)

    block = own_block(tile, chips, cells, start, 1)
    return call(
        kernel,
        place,
        [features, twin, partial],
        [
            block,
            pl.BlockSpec((tile, chips, cells, channels), lambda i, p: (i, 0, 0, 0)),
            pl.BlockSpec(memory_space=pl.ANY),
        ],
        block,
        jax.ShapeDtypeStruct(features.shape, jnp.bfloat16),
        (steps,),
        alias={3: 0},
    )


def lat_forward(part, table, place, step_cells=8):
    sources, cells, rows, channels = part.shape
    total = sources * rows
    half = total // 2

    def kernel(place_ref, x_ref, table_ref, out_ref):
        sums = lat_sums(x_ref, table_ref, step_cells)
        for t in range(2):
            lines = jnp.stack([v[t * half : (t + 1) * half] for v in sums], axis=0)
            out_ref[:, :, t * channels : (t + 1) * channels] = turn(lines)

    return call(
        kernel,
        place,
        [part, table],
        [
            pl.BlockSpec((sources, step_cells, rows, channels), lambda i, p: (0, i, 0, 0)),
            pl.BlockSpec((total, total), lambda i, p: (0, 0)),
        ],
        pl.BlockSpec((half, step_cells, 2 * channels), lambda i, p: (0, i, 0)),
        jax.ShapeDtypeStruct((half, cells, 2 * channels), jnp.bfloat16),
        (cells // step_cells,),
    )


def lat_sums(x_ref, table_ref, cells):
    sources, channels = x_ref.shape[0], x_ref.shape[3]
    sums = []
    for cell in range(0, cells, 2):
        pair = [jnp.concatenate([x_ref[j, cell + t] for j in range(sources)], axis=0) for t in range(2)]
        result = dot32(table_ref[...], jnp.concatenate(pair, axis=1)).astype(jnp.bfloat16)
        sums += [result[:, :channels], result[:, channels:]]
    return sums


def lat_forward_groups(part, table, place, groups):
    sources, cells, rows, channels = part.shape
    total = sources * rows
    half = total // 2
    size = half // groups

    def kernel(place_ref, x_ref, table_ref, *refs):
        outs, stage = refs[:-1], refs[-1]
        for cell, value in enumerate(lat_sums(x_ref, table_ref, cells)):
            stage[:, :, cell] = value.reshape(2, groups, size, channels)
        for e in range(groups):
            for t in range(2):
                outs[e][:, :, t * channels : (t + 1) * channels] = turn(stage[t, place_ref[2] ^ e])

    shape = (size, cells, 2 * channels)
    return call(
        kernel,
        place,
        [part, table],
        [pl.BlockSpec(part.shape, lambda i, p: (0, 0, 0, 0)), pl.BlockSpec((total, total), lambda i, p: (0, 0))],
        [pl.BlockSpec(shape, lambda i, p: (0, 0, 0))] * groups,
        [jax.ShapeDtypeStruct(shape, jnp.bfloat16)] * groups,
        (1,),
        [pltpu.VMEM((2, groups, cells, size, channels), jnp.bfloat16)],
    )


def lat_back(h, table, place, groups, count, step_cells=8):
    half, cells, width = h.shape
    channels = width // 2
    total = 2 * half
    rows = total // groups // count

    def kernel(place_ref, h_ref, table_ref, *outs):
        lines = [turn(h_ref[:, :, part * channels : (part + 1) * channels]) for part in range(2)]
        for cell in range(0, step_cells, 2):
            pair = [jnp.concatenate([v[cell + t] for v in lines], axis=0) for t in range(2)]
            result = dot32(table_ref[...], jnp.concatenate(pair, axis=1)).astype(jnp.bfloat16)
            for t in range(2):
                part = result[:, t * channels : (t + 1) * channels].reshape(count, groups, rows, channels)
                for d in range(count):
                    outs[d][:, cell + t] = part[d]

    return call(
        kernel,
        place,
        [h, table],
        [
            pl.BlockSpec((half, step_cells, width), lambda i, p: (0, i, 0)),
            pl.BlockSpec((total, total), lambda i, p: (0, 0)),
        ],
        [pl.BlockSpec((groups, step_cells, rows, channels), lambda i, p: (0, i, 0, 0))] * count,
        [jax.ShapeDtypeStruct((groups, cells, rows, channels), jnp.bfloat16)] * count,
        (cells // step_cells,),
    )


def merge(chunks, place):
    count, groups = len(chunks), len(chunks[0])
    targets, slots, cells, width = chunks[0][0].shape

    def kernel(place_ref, *refs):
        ins, outs = refs[: count * groups], refs[count * groups :]
        for d in range(targets):
            for c in range(count):
                for e in range(groups):
                    outs[d][e, :, c * cells : (c + 1) * cells] = ins[c * groups + e][place_ref[0] ^ d]

    shape = (groups, slots, count * cells, width)
    return call(
        kernel,
        place,
        [v for chunk in chunks for v in chunk],
        [pl.BlockSpec(chunks[0][0].shape, lambda i, p: (0, 0, 0, 0))] * (count * groups),
        [pl.BlockSpec(shape, lambda i, p: (0, 0, 0, 0))] * targets,
        [jax.ShapeDtypeStruct(shape, jnp.bfloat16)] * targets,
        (1,),
    )


def whole(array):
    return pl.BlockSpec(array.shape, lambda i, p: (0,) * array.ndim)


def spectral_step(parts, chunk, place, fwd, inv, w1, b1, w2, b2, together=2):
    targets = len(parts)
    groups, slots, cells, width = parts[0].shape
    channels = width // 2
    sources, _, more, _ = chunk.shape
    first = targets * groups * cells // 2
    keep = fwd.shape[1] // 2

    def kernel(place_ref, *refs):
        ins, g_ref, refs = refs[:targets], refs[targets], refs[targets + 1 :]
        fwd_ref, inv_ref, w1_ref, b1_ref, w2_ref, b2_ref = refs[:6]
        near_ref, out_ref, stage = refs[6:]
        pairs = [(d, e) for d in range(targets) for e in range(groups)]

        def waves(u):
            for d, e in pairs:
                stage[u, place_ref[0] ^ d, place_ref[2] ^ e] = ins[d][e, u]
            near = stage[u]
            far = g_ref[:, u].reshape(targets, groups, more, width)
            halves = [
                jnp.concatenate([v[:, z : z + groups // 2].reshape(-1, width) for v in (near, far)], axis=0)
                for z in (0, groups // 2)
            ]
            return [dot32(fwd_ref[0], halves[0] + halves[1]), dot32(fwd_ref[1], halves[0] - halves[1])]

        def mix(u, both):
            cc, sc = both[:keep, :channels], both[:keep, channels:]
            cs, ss = both[keep:, :channels], both[keep:, channels:]
            single = (place_ref[1] + pl.program_id(0) * together + u) == 0
            upper = [jnp.where(single, cc, cc + ss), jnp.where(single, cs, cs - sc)]
            lower = [jnp.where(single, sc, cc - ss), jnp.where(single, ss, cs + sc)]
            modes = [jnp.concatenate([v.astype(jnp.bfloat16) for v in part], axis=1) for part in (upper, lower)]
            modes = jnp.concatenate(modes, axis=0)
            hidden = jnp.maximum((dot32(modes, w1_ref[...]) + b1_ref[...]).astype(jnp.bfloat16), 0)
            value = dot32(hidden, w2_ref[...]) + b2_ref[...]
            mixed = value - jnp.clip(value, -shrink_level, shrink_level)
            a, b = mixed[:keep, :channels], mixed[:keep, channels:]
            c, d = mixed[keep:, :channels], mixed[keep:, channels:]
            cos_part = [jnp.where(single, a, a + c), jnp.where(single, c, d - b)]
            sin_part = [jnp.where(single, b, b + d), jnp.where(single, d, a - c)]
            coefs = [jnp.concatenate([v.astype(jnp.bfloat16) for v in part], axis=1) for part in (cos_part, sin_part)]
            return jnp.concatenate(coefs, axis=0)

        def back(u, coefs):
            even, odd = dot32(inv_ref[0], coefs[0]), dot32(inv_ref[1], coefs[1])
            halves = [(even + odd).astype(jnp.bfloat16), (even - odd).astype(jnp.bfloat16)]
            for ref, rows in ((near_ref, slice(0, first)), (out_ref, slice(first, None))):
                parts = [v[rows].reshape(targets, groups // 2, -1, width) for v in halves]
                ref[:, u] = jnp.concatenate(parts, axis=1).reshape(sources, -1, width)

        both = [waves(u) for u in range(together)]
        coefs = [[mix(u, v) for v in both[u]] for u in range(together)]
        for u in range(together):
            back(u, coefs[u])

    near = pl.BlockSpec((groups, together, cells, width), lambda i, p: (0, i, 0, 0))
    block = pl.BlockSpec((sources, together, more, width), lambda i, p: (0, i, 0, 0))
    tables = [fwd, inv, w1, b1, w2, b2]
    return call(
        kernel,
        place,
        [*parts, chunk, *tables],
        [near] * targets + [block] + [whole(v) for v in tables],
        [pl.BlockSpec((sources, together, cells, width), lambda i, p: (0, i, 0, 0)), block],
        [jax.ShapeDtypeStruct((sources, slots, n, width), jnp.bfloat16) for n in (cells, more)],
        (slots // together,),
        [pltpu.VMEM((together, targets, groups, cells, width), jnp.bfloat16)],
        mib=62,
    )
def complex_weights(weights):
    real, imag = weights[0, 0], weights[1, 0]
    return jnp.concatenate(
        [jnp.concatenate([real, imag], axis=1), jnp.concatenate([-imag, real], axis=1)], axis=0
    )


def swap(parts, axis):
    return [parts[0]] + [swap_bits(parts[d], axis, d) for d in range(1, len(parts))]


def swap_bits(part, axis, bits):
    return lax.ppermute(part, axis, [(j, j ^ bits) for j in range(lax.axis_size(axis))])


def swap_chips(parts):
    return [parts[0]] + [swap_bits(parts[d], "lat", 2 * d) for d in range(1, len(parts))]


def swap_lat(parts):
    return lax.all_to_all(parts, "lat", split_axis=0, concat_axis=0, tiled=True)


def swap_all(parts):
    return lax.all_to_all(parts, ("lat", "lon"), split_axis=0, concat_axis=0, tiled=True)


def lat_first_body(features, w_first, bias_first, w_second, bias_second):
    rows, lon_cells, channels = features.shape
    lat_count, lon_count = lax.axis_size("lat"), lax.axis_size("lon")
    total_lat, total_lon = rows * lat_count, lon_cells * lon_count
    devices, width = lat_count * lon_count, 2 * channels
    block_cells = lon_cells // lat_count
    slots = total_lat // 2 // devices
    norm = 1.0 / math.sqrt(total_lat * total_lon)
    half = block_cells // 2
    sizes, starts = [half // 2, half // 2, half], [0, half // 2, half]
    cell_index = np.arange(total_lon).reshape(lon_count, lat_count, 2, half).transpose(2, 1, 0, 3)
    cell_index = cell_index[:, :, : lon_count // 2]
    lon_fwd, lon_inv = lon_tables(cell_index.reshape(-1), total_lon, norm)
    slot_l = np.arange(total_lat // 2)
    lat_fwd, lat_inv = lat_tables(total_lat, norm, slot_l)
    by_lon = slot_l.reshape(lat_count, lon_count, slots).transpose(1, 0, 2).reshape(-1)
    lon_first_fwd, _ = lat_tables(total_lat, norm, by_lon)
    places = np.arange(lat_count)
    by_place = lat_inv.reshape(lat_count, rows, total_lat)
    own_inv = np.stack([by_place[p ^ places].reshape(lat_inv.shape) for p in range(lat_count)])
    lat_place, lon_place = lax.axis_index("lat"), lax.axis_index("lon")
    first_slot = (lat_place * lon_count + lon_place) * slots
    place = jnp.stack([lat_place, first_slot, lon_place]).astype(jnp.int32)
    own_inv = lax.dynamic_index_in_dim(jnp.asarray(own_inv), lat_place, 0, keepdims=False)
    w1, w2 = complex_weights(w_first), complex_weights(w_second)
    b1, b2 = bias_first.reshape(1, -1), bias_second.reshape(1, -1)
    tie = lax.optimization_barrier
    field = features.reshape(rows, lat_count // 2, 2, block_cells, channels)

    sent = split_all(tie(field[:, :, :, : sizes[0]]), place, 0, sizes[0], 2)
    later, sent = tie((field, sent))
    waiting = [split_all(later, place, starts[i], sizes[i]) for i in (1, 2)]
    got, waiting = tie((swap_lat(sent), waiting))
    across = []
    for i in range(2):
        groups = lat_forward_groups(got, lon_first_fwd, place, lon_count)
        sent, groups = tie((waiting[i], groups))
        if across:
            sent, across[-1] = tie((sent, across[-1]))
        got = swap_lat(sent)
        across.append(swap(groups, "lon"))
    last = lat_forward(got, lat_fwd, place)
    last, across[-1] = tie((last, across[-1]))
    last = swap_all(last.reshape(devices, slots, sizes[2], width))
    near = [[v.reshape(lat_count, slots, sizes[0], width) for v in groups] for groups in across]
    near = swap(merge(near, place), "lat")

    near, last = spectral_step(near, last, place, lon_fwd, lon_inv, w1, b1, w2, b2)

    last = swap_all(last).reshape(devices * slots, half, width)
    last = swap_chips(lat_back(last, own_inv, place, 2, lat_count // 2))
    near = swap_all(near).reshape(devices * slots, half, width)
    near, last = tie((near, last))
    near = lat_back(near, lat_inv, place, lat_count, 1)[0]
    near, last = tie((near, last))
    near = swap_lat(near)
    result, for_twin = join_own(field, last, place, half, None)
    result = join_twin(field, swap_bits(for_twin, "lat", 1), place, half, result)
    result = join_all(field, near, place, 0, result)
    return result.reshape(features.shape)


def body(features, w_first, bias_first, w_second, bias_second):
    rows, lon_cells, channels = features.shape
    lat_count, lon_count = lax.axis_size("lat"), lax.axis_size("lon")
    fits = (
        (rows * lat_count) % (4 * lat_count * lon_count) == 0
        and lat_count & (lat_count - 1) == 0
        and lat_count > 1
        and lon_cells % (32 * lat_count) == 0
        and lon_count & (lon_count - 1) == 0
        and lon_count > 1
        and rows % 64 == 0
        and channels == 128
        and w_first.shape[1] == 1
    )
    chosen = lat_first_body if fits else general_body
    return chosen(features, w_first, bias_first, w_second, bias_second)


def solution(mesh):
    in_specs = (P("lat", "lon", None), P(), P(), P(), P())
    out_specs = P("lat", "lon", None)
    return jax.shard_map(body, mesh=mesh, in_specs=in_specs, out_specs=out_specs, check_vma=False)
```
